256 devices in a mesh: dcn: 2 (over core), gx: 8 (over z_lo, y), gy: 4 (over z_hi), gz: 4 (over x).
Axes of the slice: x: 4, y: 4, z: 8 (z_hi: 4, z_lo: 2; z = z_hi * 2 + z_lo), core: 2. Of those that a mesh axis runs over, the one named last changes fastest.
Arguments:
- tokens: bfloat16 [512, 8192], P(('dcn', 'gx', 'gz'), 'gy'), may hold values from -6 to 6
- gate_weight: bfloat16 [28672, 8192], P(('dcn', 'gx', 'gz'), 'gy'), may hold values from -0.0625 to 0.0625
- up_weight: bfloat16 [28672, 8192], P(('dcn', 'gx', 'gz'), 'gy'), may hold values from -0.0625 to 0.0625
- down_weight: bfloat16 [28672, 8192], P(('dcn', 'gx', 'gz'), 'gy'), may hold values from -0.03125 to 0.03125
- out_grad: bfloat16 [512, 8192], P(('dcn', 'gx', 'gz'), 'gy'), may hold values from -6 to 6
Outputs:
- output: bfloat16 [512, 8192], P(('dcn', 'gx', 'gz'), 'gy')
- tokens_grad: bfloat16 [512, 8192], P(('dcn', 'gx', 'gz'), 'gy')
- gate_grad: bfloat16 [28672, 8192], P(('dcn', 'gx', 'gz'), 'gy')
- up_grad: bfloat16 [28672, 8192], P(('dcn', 'gx', 'gz'), 'gy')
- down_grad: bfloat16 [28672, 8192], P(('dcn', 'gx', 'gz'), 'gy')
The draws below stay inside these ranges and needn't reach their ends.
All inputs are finite; a program needn't handle non-finite values.
Results may differ from the reference program's by a relative error of at most 0.0054.
Values may be sent and summed in bfloat16 or wider, within the bound.
No kernel may reach another device: no remote copies, remote signals or barrier semaphores. Data moves between devices by JAX's collectives and lax.ppermute only.
A program may use at most 128 MiB of HBM per device.

```python
import math
import jax
import jax.numpy as jnp

D = 8192
FF = 28672
ALL_TOK = 512


def levels(rng, shape, cuts, least, top_value):
    gain = 1.0
    for axis_at, shards_of in cuts:
        draws = jax.random.uniform(jax.random.fold_in(jax.random.fold_in(rng, 6), axis_at), (shards_of,), jnp.float32, least / len(cuts), top_value / len(cuts))
        gain = gain * jnp.repeat(jnp.exp(draws), shape[axis_at] // shards_of).reshape((-1,) + (1,) * (len(shape) - 1 - axis_at))
    return gain


def centred(key, extent, width, most, pieces=(), held_as=jnp.bfloat16):
    result = jax.random.normal(key, extent, jnp.float32) * width
    if len(pieces) > 0:
        result = levels(key, extent, pieces, -0.22, 0.18) * result
    return jnp.clip(result, min=-most, max=most).astype(held_as)


def setup_inputs(seed: int = 0) -> dict:
    key_list = jax.random.split(jax.random.key(seed), 6)
    tokens = centred(key_list[0], (ALL_TOK, D), 1.0, 6.0, ((0, 64), (1, 4)))
    gate_weight = centred(key_list[1], (FF, D), D ** -0.5, 0.0625, ((0, 64), (1, 4)))
    up_weight = centred(key_list[2], (FF, D), D ** -0.5, 0.0625, ((0, 64), (1, 4)))
    down_weight = centred(key_list[3], (FF, D), FF ** -0.5, 0.03125, ((0, 64), (1, 4)))
    out_grad = centred(key_list[4], (ALL_TOK, D), 1.0, 6.0, ((0, 64), (1, 4)))
    return dict(tokens=tokens, gate_weight=gate_weight, up_weight=up_weight, down_weight=down_weight, out_grad=out_grad)


def reference(tokens, gate_weight, up_weight, down_weight, out_grad):
    factor = 1.0 / math.sqrt(ALL_TOK)
    gate_value = jnp.dot(tokens, gate_weight.T, preferred_element_type=jnp.float32)
    up_value = jnp.dot(tokens, up_weight.T, preferred_element_type=jnp.float32)
    sigmoid_gate = jax.nn.sigmoid(gate_value)
    hidden = (gate_value * sigmoid_gate * up_value).astype(jnp.bfloat16)
    output = jnp.dot(hidden, down_weight, preferred_element_type=jnp.float32).astype(jnp.bfloat16)
    hidden_grad = jnp.dot(out_grad, down_weight.T, preferred_element_type=jnp.float32)
    gate_delta = (hidden_grad * up_value * sigmoid_gate * (1.0 + gate_value * (1.0 - sigmoid_gate))).astype(jnp.bfloat16)
    up_delta = (hidden_grad * gate_value * sigmoid_gate).astype(jnp.bfloat16)
    tokens_grad = (jnp.dot(gate_delta, gate_weight, preferred_element_type=jnp.float32) + jnp.dot(up_delta, up_weight, preferred_element_type=jnp.float32)).astype(jnp.bfloat16)
    gate_grad = (jnp.dot(gate_delta.T, tokens, preferred_element_type=jnp.float32) * factor).astype(jnp.bfloat16)
    up_grad = (jnp.dot(up_delta.T, tokens, preferred_element_type=jnp.float32) * factor).astype(jnp.bfloat16)
    down_grad = (jnp.dot(hidden.T, out_grad, preferred_element_type=jnp.float32) * factor).astype(jnp.bfloat16)
    return (output, tokens_grad, gate_grad, up_grad, down_grad)
```

```python
import math

import jax
import jax.numpy as jnp
from jax import lax
from jax.experimental import pallas as pl
from jax.experimental.pallas import tpu as pltpu
from jax.sharding import PartitionSpec as P

BF16, F32 = jnp.bfloat16, jnp.float32
PLANE = ("gx", "gz")
WIDTH = 512
SMEM = pl.BlockSpec(memory_space=pltpu.SMEM)
VMEM = pl.BlockSpec(memory_space=pltpu.VMEM)
PARAMS = pltpu.CompilerParams(vmem_limit_bytes=40 * 1024 * 1024)


def by_features(left, right):
    return lax.dot_general(left, right, (((1,), (1,)), ((), ())), preferred_element_type=F32)


def cost(flops, moved):
    return pl.CostEstimate(flops=int(flops), bytes_accessed=int(moved), transcendentals=0)


def shifted(x, axis, by):
    n = lax.axis_size(axis)
    return lax.ppermute(x, axis, [(i, (i + by) % n) for i in range(n)])


def partial_sums(me, own, other, weights):
    count, ways = len(weights), 4
    units, width = weights[0].shape
    rows = own.shape[0]
    block = 2 * rows // ways

    def kernel(me_ref, own_ref, other_ref, *refs):
        w_refs, o_refs, held = refs[:count], refs[count : count + ways], refs[-1]
        for k in range(count):
            for half, t_ref in enumerate((own_ref, other_ref)):
                sums = by_features(w_refs[k][...], t_ref[...])
                held[2 * half, k] = sums[:, :block]
                held[2 * half + 1, k] = sums[:, block:]
        for s in range(ways):
            o_refs[s][...] = held[lax.rem(me_ref[0] + s, ways)].astype(o_refs[s].dtype)

    shape = (count, units, block)
    return pl.pallas_call(
        kernel,
        in_specs=[SMEM] + [VMEM] * (2 + count),
        out_specs=[VMEM] * ways,
        out_shape=[jax.ShapeDtypeStruct(shape, F32 if s == 0 else BF16) for s in range(ways)],
        scratch_shapes=[pltpu.VMEM((ways,) + shape, F32)],
        compiler_params=PARAMS,
        cost_estimate=cost(4 * count * units * width * rows, 2 * width * (2 * rows + count * units)),
        name="partial_sums",
    )(me, own, other, *weights)


def row_sums(me, blocks, weights):
    count, ways = len(weights), 4
    units, width = weights[0].shape
    block = blocks[0].shape[-1]

    def kernel(me_ref, *refs):
        b_refs, w_refs = refs[:ways], refs[ways : ways + count]
        own_ref, other_ref, held = refs[ways + count :]

        @pl.when(pl.program_id(0) == 0)
        def _():
            for s in range(ways):
                at = pl.multiple_of(lax.rem(me_ref[0] + s, ways) * block, block)
                for k in range(count):
                    held[pl.ds(at, block), k * units : (k + 1) * units] = b_refs[s][k].T

        total = 0.0
        for k in range(count):
            total += jnp.dot(
                held[:, k * units : (k + 1) * units], w_refs[k][...], preferred_element_type=F32
            )
        own_ref[...] = total[: 2 * block]
        other_ref[...] = total[2 * block :].astype(BF16)

    columns = pl.BlockSpec((units, WIDTH), lambda i: (0, i))
    rows = pl.BlockSpec((2 * block, WIDTH), lambda i: (0, i))
    return pl.pallas_call(
        kernel,
        grid=(width // WIDTH,),
        in_specs=[SMEM] + [VMEM] * ways + [columns] * count,
        out_specs=[rows, rows],
        out_shape=[
            jax.ShapeDtypeStruct((2 * block, width), F32),
            jax.ShapeDtypeStruct((2 * block, width), BF16),
        ],
        scratch_shapes=[pltpu.VMEM((ways * block, count * units), BF16)],
        compiler_params=PARAMS,
        cost_estimate=cost(2 * ways * block * count * units * width, 2 * width * (count * units + 6 * block)),
        name="row_sums",
    )(me, *blocks, *weights)


def weight_grads(me, blocks, own, other, factor):
    ways = 4
    count, units, block = blocks[0].shape
    width = own.shape[1]

    def kernel(me_ref, *refs):
        b_refs, (own_ref, other_ref) = refs[:ways], refs[ways : ways + 2]
        o_refs, held = refs[ways + 2 : -1], refs[-1]

        @pl.when(pl.program_id(0) == 0)
        def _():
            for s in range(ways):
                at = pl.multiple_of(lax.rem(me_ref[0] + s, ways) * block, block)
                for k in range(count):
                    held[k, :, pl.ds(at, block)] = b_refs[s][k]

        for k in range(count):
            total = jnp.dot(held[k, :, : 2 * block], own_ref[...], preferred_element_type=F32)
            total += jnp.dot(held[k, :, 2 * block :], other_ref[...], preferred_element_type=F32)
            o_refs[k][...] = (total * factor).astype(BF16)

    rows = pl.BlockSpec((2 * block, WIDTH), lambda i: (0, i))
    columns = pl.BlockSpec((units, WIDTH), lambda i: (0, i))
    return pl.pallas_call(
        kernel,
        grid=(width // WIDTH,),
        in_specs=[SMEM] + [VMEM] * ways + [rows, rows],
        out_specs=[columns] * count,
        out_shape=[jax.ShapeDtypeStruct((units, width), BF16)] * count,
        scratch_shapes=[pltpu.VMEM((count, units, ways * block), BF16)],
        compiler_params=PARAMS,
        cost_estimate=cost(2 * ways * block * count * units * width, 2 * width * (count * units + 4 * block)),
        name="weight_grads",
    )(me, *blocks, own, other)


def gathered(x):
    n = lax.axis_size("gx") * lax.axis_size("gz")
    rows, width = x.shape
    spread = jnp.broadcast_to(x[None], (n, rows, width))
    own = lax.all_to_all(spread, PLANE, 0, 0, tiled=True).reshape(n * rows, width)
    return own, shifted(own, "dcn", 1)


def scattered(own, other):
    n = lax.axis_size("gx") * lax.axis_size("gz")
    rows, width = own.shape
    both = (own + shifted(other, "dcn", 1).astype(F32)).astype(BF16)
    parts = lax.all_to_all(both.reshape(n, rows // n, width), PLANE, 0, 0, tiled=True)
    return jnp.sum(parts.astype(F32), axis=0).astype(BF16)


def exchanged(parts):
    return [parts[0]] + [shifted(parts[s], "gy", s) for s in (1, 2, 3)]


def spread(block):
    return [block] + [shifted(block, "gy", -s) for s in (1, 2, 3)]


def summed(parts):
    total = parts[0]
    for part in parts[1:]:
        total = total + part.astype(F32)
    return total


def per_device(tokens, gate_weight, up_weight, down_weight, out_grad):
    token_count = tokens.shape[0] * lax.axis_size("dcn") * lax.axis_size("gx") * lax.axis_size("gz")
    factor = 1.0 / math.sqrt(token_count)
    me = lax.axis_index("gy").astype(jnp.int32).reshape(1)

    token_rows = gathered(tokens)
    gate_up_parts = partial_sums(me, *token_rows, (gate_weight, up_weight))
    gate_up_parts = exchanged(gate_up_parts)

    out_grad, _ = lax.optimization_barrier((out_grad, token_rows[1]))
    grad_rows = gathered(out_grad)
    hgrad_parts = exchanged(partial_sums(me, *grad_rows, (down_weight,)))

    gate_total, up_total = summed(gate_up_parts)
    sigmoid_gate = jax.nn.sigmoid(gate_total)
    hidden = (gate_total * sigmoid_gate * up_total).astype(BF16)
    hidden_all = spread(hidden[None])

    hidden_grad = summed(hgrad_parts)[0]
    gate_delta = (
        hidden_grad * up_total * sigmoid_gate * (1.0 + gate_total * (1.0 - sigmoid_gate))
    ).astype(BF16)
    up_delta = (hidden_grad * gate_total * sigmoid_gate).astype(BF16)
    deltas_all = spread(jnp.stack([gate_delta, up_delta]))

    output = scattered(*row_sums(me, hidden_all, (down_weight,)))
    (down_grad,) = weight_grads(me, hidden_all, *grad_rows, factor)
    tokens_grad = scattered(*row_sums(me, deltas_all, (gate_weight, up_weight)))
    gate_grad, up_grad = weight_grads(me, deltas_all, *token_rows, factor)
    return output, tokens_grad, gate_grad, up_grad, down_grad


def solution(mesh):
    placed = P(("dcn", "gx", "gz"), "gy")
    return jax.shard_map(
        per_device,
        mesh=mesh,
        in_specs=(placed,) * 5,
        out_specs=(placed,) * 5,
        check_vma=False,
    )
```

```python
import math

import jax
import jax.numpy as jnp
from jax import lax
from jax.experimental import pallas as pl
from jax.experimental.pallas import tpu as pltpu
from jax.sharding import PartitionSpec as P

BF16, F32 = jnp.bfloat16, jnp.float32
PLANE = ("gx", "gz")
WIDTH = 512
WAYS = 4
SMEM = pl.BlockSpec(memory_space=pltpu.SMEM)
VMEM = pl.BlockSpec(memory_space=pltpu.VMEM)
HBM = pl.BlockSpec(memory_space=pltpu.HBM)
PARAMS = pltpu.CompilerParams(vmem_limit_bytes=24 * 1024 * 1024)


def local(kernel, out_shape, *args, scratch=(), flops=1e6, moved=1e6):
    return pl.pallas_call(
        kernel,
        in_specs=[SMEM if a.dtype == jnp.int32 else VMEM for a in args],
        out_specs=[VMEM] * len(out_shape),
        out_shape=[jax.ShapeDtypeStruct(*s) for s in out_shape],
        scratch_shapes=list(scratch),
        compiler_params=PARAMS,
        cost_estimate=pl.CostEstimate(flops=int(flops), bytes_accessed=int(moved), transcendentals=0),
        name=kernel.__name__,
    )(*args)


def swapped(x):
    return lax.ppermute(x, "dcn", [(0, 1), (1, 0)])


def after(x, *others):
    return lax.optimization_barrier((x, *others))[0]


def copies(tokens, out_grad, peers):
    rows, width = tokens.shape

    def copies_of(t_ref, g_ref, out_ref):
        both = jnp.concatenate([t_ref[...].astype(F32), g_ref[...].astype(F32)]).astype(BF16)
        for p in range(peers):
            out_ref[p] = both

    return local(copies_of, [((peers, 2 * rows, width), BF16)], tokens, out_grad)[0]


def parted(rows_of_peers):
    peers, rows, width = rows_of_peers.shape
    half = rows // 2

    def parted_of(in_ref, out_ref):
        for p in range(0, peers, 2):
            first, second = in_ref[p].astype(F32), in_ref[p + 1].astype(F32)
            to = slice(p * half, (p + 2) * half)
            out_ref[0, to] = jnp.concatenate([first[:half], second[:half]]).astype(BF16)
            out_ref[1, to] = jnp.concatenate([first[half:], second[half:]]).astype(BF16)

    return local(parted_of, [((2, peers * half, width), BF16)], rows_of_peers)[0]


def loaded(weights):
    def loaded_of(*refs):
        sems = refs[-1]
        moves = [pltpu.make_async_copy(refs[k], refs[3 + k], sems.at[k]) for k in range(3)]
        for move in moves:
            move.start()
        for move in moves:
            move.wait()

    shape = jax.ShapeDtypeStruct(weights[0].shape, BF16)
    return pl.pallas_call(
        loaded_of,
        in_specs=[HBM] * 3,
        out_specs=[VMEM] * 3,
        out_shape=[shape] * 3,
        scratch_shapes=[pltpu.SemaphoreType.DMA((3,))],
        compiler_params=PARAMS,
        cost_estimate=pl.CostEstimate(flops=1000000, bytes_accessed=20000000, transcendentals=0),
        name="loaded",
    )(*weights)


def partial_sums(own, other, weights):
    units, width = weights[0].shape
    rows = own.shape[1]
    block = rows // 2
    part = 3 * units // 2

    def partial_sums_of(own_ref, other_ref, w0, w1, w2, low, high, after_, before, mine, held):
        for k, w_ref in enumerate((w0, w1, w2)):
            for half, r_ref in enumerate((own_ref, other_ref)):
                sums = lax.dot_general(
                    w_ref[...],
                    r_ref[0 if k < 2 else 1],
                    (((1,), (1,)), ((), ())),
                    preferred_element_type=F32,
                )
                for c in range(2):
                    held[2 * half + c, k * units : (k + 1) * units] = sums[:, c * block : (c + 1) * block]
        me = lax.axis_index("gy")
        far = lax.rem(me + 2, WAYS)
        low[...] = held[far, :part].astype(BF16)
        high[...] = held[far, part:].astype(BF16)
        after_[...] = held[lax.rem(me + 1, WAYS)]
        before[...] = held[lax.rem(me + 3, WAYS)]
        mine[...] = held[me]

    full = ((3 * units, block), F32)
    return local(
        partial_sums_of,
        [((part, block), BF16)] * 2 + [full] * 3,
        own,
        other,
        *weights,
        scratch=[pltpu.VMEM((WAYS, 3 * units, block), F32)],
        flops=12 * units * width * rows,
    )


def shifted(x, by):
    n = lax.axis_size("gy")
    return lax.ppermute(x, "gy", [(i, (i + by) % n) for i in range(n)])


def ring_sums(low, high, following, before, mine):
    rows, block = mine.shape
    part = rows // 2
    low, high = shifted(low, 1), shifted(high, -1)

    def joined_of(low_ref, high_ref, f_ref, b_ref, f_out, b_out):
        f_out[:part] = (f_ref[:part] + low_ref[...].astype(F32)).astype(BF16)
        f_out[part:] = f_ref[part:].astype(BF16)
        b_out[:part] = b_ref[:part].astype(BF16)
        b_out[part:] = (b_ref[part:] + high_ref[...].astype(F32)).astype(BF16)

    following, before = local(joined_of, [((rows, block), BF16)] * 2, low, high, following, before)
    return shifted(following, 1), shifted(before, -1)


def activations(behind, ahead, mine):
    rows, block = mine.shape
    units = rows // 3

    def activations_of(behind_ref, ahead_ref, mine_ref, out_ref):
        def total(k):
            at = slice(k * units, (k + 1) * units)
            return mine_ref[at] + behind_ref[at].astype(F32) + ahead_ref[at].astype(F32)

        gate, up, hidden_grad = total(0), total(1), total(2)
        sigmoid = jax.nn.sigmoid(gate)
        silu = gate * sigmoid
        out_ref[:units] = (silu * up).astype(BF16)
        out_ref[units : 2 * units] = (
            hidden_grad * up * sigmoid * (1.0 + gate * (1.0 - sigmoid))
        ).astype(BF16)
        out_ref[2 * units :] = (hidden_grad * silu).astype(BF16)

    return local(activations_of, [((rows, block), BF16)], behind, ahead, mine)[0]


def ring_gather(mine):
    rows, block = mine.shape
    part = rows // 2
    behind, ahead = shifted(mine, 1), shifted(mine, -1)
    low, high = shifted(behind[:part], 1), shifted(ahead[part:], -1)

    def placed_of(mine_ref, behind_ref, ahead_ref, low_ref, high_ref, out_ref):
        me = lax.axis_index("gy")
        far = lax.rem(me + 2, WAYS)
        out_ref[me] = mine_ref[...]
        out_ref[lax.rem(me + 3, WAYS)] = behind_ref[...]
        out_ref[lax.rem(me + 1, WAYS)] = ahead_ref[...]
        out_ref[far, :part] = low_ref[...]
        out_ref[far, part:] = high_ref[...]

    return local(
        placed_of, [((WAYS, rows, block), BF16)], mine, behind, ahead, low, high
    )[0]


def row_sums(blocks, weights, half, dtype):
    _, rows, block = blocks.shape
    units, width = weights[0].shape

    def row_sums_of(b_ref, w0, w1, w2, out_ref, held):
        for c in range(2):
            for k in range(3):
                at = slice(k * units, (k + 1) * units)
                held[k, c * block : (c + 1) * block] = b_ref[2 * half + c, at].T
        for p in range(width // WIDTH):
            at = slice(p * WIDTH, (p + 1) * WIDTH)
            dot = lambda k, w: jnp.dot(held[k], w[:, at], preferred_element_type=F32)
            out_ref[0, :, at] = dot(0, w2).astype(dtype)
            out_ref[1, :, at] = (dot(1, w0) + dot(2, w1)).astype(dtype)

    return local(
        row_sums_of,
        [((2, 2 * block, width), dtype)],
        blocks,
        *weights,
        scratch=[pltpu.VMEM((3, 2 * block, units), BF16)],
        flops=12 * block * units * width,
    )[0]


def merged(own, other, peers):
    _, rows, width = own.shape
    each = rows // peers

    def merged_of(own_ref, other_ref, out_ref):
        for p in range(0, peers, 2):
            at = slice(p * each, (p + 2) * each)
            out, grad = (own_ref[k, at] + other_ref[k, at].astype(F32) for k in range(2))
            out_ref[p] = jnp.concatenate([out[:each], grad[:each]]).astype(BF16)
            out_ref[p + 1] = jnp.concatenate([out[each:], grad[each:]]).astype(BF16)

    return local(merged_of, [((peers, 2 * each, width), BF16)], own, other)[0]


def totals(parts):
    peers, rows, width = parts.shape

    def totals_of(parts_ref, out_ref, grad_ref):
        for at in range(0, width, WIDTH):
            columns = slice(at, at + WIDTH)
            total = parts_ref[0, :, columns].astype(F32)
            for p in range(1, peers):
                total += parts_ref[p, :, columns].astype(F32)
            out_ref[:, columns] = total[: rows // 2].astype(BF16)
            grad_ref[:, columns] = total[rows // 2 :].astype(BF16)

    return local(totals_of, [((rows // 2, width), BF16)] * 2, parts)


def weight_grads(blocks, own, other, factor):
    _, rows, block = blocks.shape
    units, width = rows // 3, own.shape[2]

    def weight_grads_of(b_ref, own_ref, other_ref, gate_ref, up_ref, down_ref, held):
        @pl.when(pl.program_id(0) == 0)
        def _():
            for k in range(3):
                for c in range(WAYS):
                    at = slice(k * units, (k + 1) * units)
                    held[k, :, c * block : (c + 1) * block] = b_ref[c, at]

        for k, kind, out_ref in ((0, 1, down_ref), (1, 0, gate_ref), (2, 0, up_ref)):
            total = jnp.dot(held[k, :, : 2 * block], own_ref[kind], preferred_element_type=F32)
            total += jnp.dot(held[k, :, 2 * block :], other_ref[kind], preferred_element_type=F32)
            out_ref[...] = (total * factor).astype(BF16)

    token_rows = pl.BlockSpec((2, 2 * block, WIDTH), lambda i: (0, 0, i))
    columns = pl.BlockSpec((units, WIDTH), lambda i: (0, i))
    return pl.pallas_call(
        weight_grads_of,
        grid=(width // WIDTH,),
        in_specs=[VMEM, token_rows, token_rows],
        out_specs=[columns] * 3,
        out_shape=[jax.ShapeDtypeStruct((units, width), BF16)] * 3,
        scratch_shapes=[pltpu.VMEM((3, units, WAYS * block), BF16)],
        compiler_params=PARAMS,
        cost_estimate=pl.CostEstimate(
            flops=24 * block * units * width, bytes_accessed=6 * units * width, transcendentals=0
        ),
        name="weight_grads",
    )(blocks, own, other)


def per_device(tokens, gate_weight, up_weight, down_weight, out_grad):
    rows, width = tokens.shape
    peers = lax.axis_size("gx") * lax.axis_size("gz")
    factor = 1.0 / math.sqrt(rows * lax.axis_size("dcn") * peers)
    weights = (gate_weight, up_weight, down_weight)

    both = copies(tokens, out_grad, peers)
    own = parted(lax.all_to_all(both, PLANE, 0, 0, tiled=True))
    other = swapped(own)
    sums = partial_sums(own, other, weights)
    mine = activations(*ring_sums(*sums), sums[-1])
    blocks = ring_gather(mine)

    theirs = row_sums(blocks, weights, 1, BF16)
    ours = row_sums(after(blocks, theirs), weights, 0, F32)
    merged_rows = merged(ours, swapped(theirs), peers)
    parts = lax.all_to_all(merged_rows, PLANE, 0, 0, tiled=True)
    gate_grad, up_grad, down_grad = weight_grads(after(blocks, merged_rows), own, other, factor)
    output, tokens_grad = totals(parts)
    return output, tokens_grad, gate_grad, up_grad, down_grad


def solution(mesh):
    placed = P(("dcn", "gx", "gz"), "gy")
    return jax.shard_map(
        per_device,
        mesh=mesh,
        in_specs=(placed,) * 5,
        out_specs=(placed,) * 5,
        check_vma=False,
    )
```

```python
import math

import jax
import jax.numpy as jnp
from jax import lax
from jax.experimental import pallas as pl
from jax.experimental.pallas import tpu as pltpu
from jax.sharding import PartitionSpec as P

BF16, F32 = jnp.bfloat16, jnp.float32
CUBE = ("dcn", "gx", "gz")
NEAR = 2
WIDTH = 512
WAYS = 4
SMEM = pl.BlockSpec(memory_space=pltpu.SMEM)
VMEM = pl.BlockSpec(memory_space=pltpu.VMEM)
PARAMS = pltpu.CompilerParams(vmem_limit_bytes=24 * 1024 * 1024)


def local(kernel, out_shape, *args, scratch=(), flops=1e6, moved=1e6):
    return pl.pallas_call(
        kernel,
        in_specs=[SMEM if a.dtype == jnp.int32 else VMEM for a in args],
        out_specs=[VMEM] * len(out_shape),
        out_shape=[jax.ShapeDtypeStruct(*s) for s in out_shape],
        scratch_shapes=list(scratch),
        compiler_params=PARAMS,
        cost_estimate=pl.CostEstimate(flops=int(flops), bytes_accessed=int(moved), transcendentals=0),
        name=kernel.__name__,
    )(*args)


def swapped(x):
    return lax.ppermute(x, "dcn", [(0, 1), (1, 0)])


def after(x, *others):
    return lax.optimization_barrier((x, *others))[0]


def copies(tokens, out_grad, peers):
    rows, width = tokens.shape

    def copies_of(t_hbm, g_hbm, out_ref, t_ref, g_ref, sems):
        moves = [
            pltpu.make_async_copy(t_hbm, t_ref, sems.at[0]),
            pltpu.make_async_copy(g_hbm, g_ref, sems.at[1]),
        ]
        for move in moves:
            move.start()
        for move in moves:
            move.wait()
        both = jnp.concatenate([t_ref[...].astype(F32), g_ref[...].astype(F32)]).astype(BF16)
        for p in range(peers):
            out_ref[p] = both

    in_hbm = pl.BlockSpec(memory_space=pltpu.HBM)
    return pl.pallas_call(
        copies_of,
        in_specs=[in_hbm] * 2,
        out_specs=VMEM,
        out_shape=jax.ShapeDtypeStruct((peers, 2 * rows, width), BF16),
        scratch_shapes=[pltpu.VMEM((rows, width), BF16)] * 2 + [pltpu.SemaphoreType.DMA((2,))],
        compiler_params=PARAMS,
        name="copies",
    )(*(pltpu.with_memory_space_constraint(x, pltpu.HBM) for x in (tokens, out_grad)))


def parted(rows_of_peers):
    peers, rows, width = rows_of_peers.shape
    half = rows // 2

    def parted_of(in_ref, t_ref, g_ref):
        for p in range(0, peers, 2):
            first, second = in_ref[p].astype(F32), in_ref[p + 1].astype(F32)
            to = slice(p * half, (p + 2) * half)
            t_ref[to] = jnp.concatenate([first[:half], second[:half]]).astype(BF16)
            g_ref[to] = jnp.concatenate([first[half:], second[half:]]).astype(BF16)

    return local(parted_of, [((peers * half, width), BF16)] * 2, rows_of_peers)


def stacked(*blocks):
    rows, width = blocks[0].shape

    def stacked_of(*refs):
        for k, ref in enumerate(refs[:-1]):
            refs[-1][k * rows : (k + 1) * rows] = ref[...]

    return local(stacked_of, [((len(blocks) * rows, width), BF16)], *blocks)[0]


def sums_into(held, first, w_ref, own_ref, other_ref):
    units, block = w_ref.shape[0], held.shape[-1]
    for half, rows_ref in enumerate((own_ref, other_ref)):
        sums = lax.dot_general(
            w_ref[...], rows_ref[...], (((1,), (1,)), ((), ())), preferred_element_type=F32
        )
        for c in range(2):
            held[2 * half + c, first : first + units] = sums[:, c * block : (c + 1) * block]


def gate_up_sums(own, other, gate, up):
    units, width = gate.shape
    rows = own.shape[0]

    def gate_up_sums_of(own_ref, other_ref, gate_ref, up_ref, out_ref):
        sums_into(out_ref, 0, gate_ref, own_ref, other_ref)
        sums_into(out_ref, units, up_ref, own_ref, other_ref)

    return local(
        gate_up_sums_of,
        [((WAYS, 2 * units, rows // 2), F32)],
        own,
        other,
        gate,
        up,
        flops=8 * units * width * rows,
    )[0]


def ring_blocks(gate_up, own, other, down):
    units, width = down.shape
    rows, block = own.shape[0], gate_up.shape[-1]
    part = 3 * units // 2

    def ring_blocks_of(gu_ref, own_ref, other_ref, w_ref, forth, back, next_, before, mine, held):
        sums_into(held, 0, w_ref, own_ref, other_ref)
        me = lax.axis_index("gy")
        after_, far, last = (lax.rem(me + s, WAYS) for s in (1, 2, 3))
        split = 2 * units - part

        def upper(ref, first, at):
            ref[first : first + split] = gu_ref[at, part:].astype(ref.dtype)
            ref[first + split : first + part] = held[at].astype(ref.dtype)

        forth[:part] = gu_ref[far, :part].astype(BF16)
        upper(forth, part, after_)
        upper(back, 0, far)
        back[part:] = gu_ref[last, :part].astype(BF16)
        next_[...] = gu_ref[after_, :part]
        upper(before, 0, last)
        mine[:part] = gu_ref[me, :part]
        upper(mine, part, me)

    full = (3 * units, block)
    return local(
        ring_blocks_of,
        [(full, BF16)] * 2 + [((part, block), F32)] * 2 + [(full, F32)],
        gate_up,
        own,
        other,
        down,
        scratch=[pltpu.VMEM((WAYS, units, block), F32)],
        flops=4 * units * width * rows,
    )


def shifted(x, by):
    n = lax.axis_size("gy")
    return lax.ppermute(x, "gy", [(i, (i + by) % n) for i in range(n)])


def plane():
    cores, ys, zs = lax.axis_size("dcn"), lax.axis_size("gx") // NEAR, lax.axis_size("gz")
    return cores, ys, zs, lambda d, n, y, z: ((d * NEAR + n) * ys + y) * zs + z


def first_groups():
    cores, ys, zs, place = plane()
    by_z = [[place(0, n, y, z) for n in range(NEAR) for z in range(zs)] for y in range(ys)]
    by_y = [[place(1, n, y, z) for n in range(NEAR) for y in range(ys)] for z in range(zs)]
    return by_z + by_y


def first_exchange(x):
    return lax.all_to_all(x, CUBE, 0, 0, axis_index_groups=first_groups(), tiled=True)


def turned(x, by):
    cores, ys, zs, place = plane()
    pairs = []
    for n in range(NEAR):
        for y in range(ys):
            for z in range(zs):
                pairs.append((place(0, n, y, z), place(0, n, (y + by) % ys, z)))
                pairs.append((place(1, n, y, z), place(1, n, y, (z + by) % zs)))
    return lax.ppermute(x, CUBE, pairs)


def ring_sums(forth, back, following, before):
    rows, block = forth.shape
    part = rows // 2
    behind, ahead = shifted(forth, 1), shifted(back, -1)

    def joined_of(here_ref, there_ref, out_ref):
        out_ref[...] = (here_ref[...] + there_ref[:part].astype(F32)).astype(BF16)

    def joined(here, there):
        return local(joined_of, [((part, block), BF16)], here, there)[0]

    low, high = shifted(joined(following, behind), 1), shifted(joined(before, ahead), -1)
    return behind, ahead, low, high


def activations(behind, ahead, low, high, mine):
    rows, block = mine.shape
    units, part = rows // 3, rows // 2

    def activations_of(behind_ref, ahead_ref, low_ref, high_ref, mine_ref, out_ref, total):
        total[:part] = (
            mine_ref[:part] + low_ref[...].astype(F32) + ahead_ref[part:].astype(F32)
        )
        total[part:] = (
            mine_ref[part:] + high_ref[...].astype(F32) + behind_ref[part:].astype(F32)
        )
        gate, up, hidden_grad = (total[k * units : (k + 1) * units] for k in range(3))
        sigmoid = jax.nn.sigmoid(gate)
        silu = gate * sigmoid
        out_ref[:units] = (silu * up).astype(BF16)
        out_ref[units : 2 * units] = (
            hidden_grad * up * sigmoid * (1.0 + gate * (1.0 - sigmoid))
        ).astype(BF16)
        out_ref[2 * units :] = (hidden_grad * silu).astype(BF16)

    return local(
        activations_of,
        [((rows, block), BF16)],
        behind,
        ahead,
        low,
        high,
        mine,
        scratch=[pltpu.VMEM((rows, block), F32)],
    )[0]


def ring_gather(mine):
    rows, block = mine.shape
    part = rows // 2
    behind, ahead = shifted(mine, 1), shifted(mine, -1)
    low, high = shifted(behind[:part], 1), shifted(ahead[part:], -1)

    def placed_of(mine_ref, behind_ref, ahead_ref, low_ref, high_ref, out_ref):
        me = lax.axis_index("gy")
        far = lax.rem(me + 2, WAYS)
        out_ref[me] = mine_ref[...]
        out_ref[lax.rem(me + 3, WAYS)] = behind_ref[...]
        out_ref[lax.rem(me + 1, WAYS)] = ahead_ref[...]
        out_ref[far, :part] = low_ref[...]
        out_ref[far, part:] = high_ref[...]

    return local(
        placed_of, [((WAYS, rows, block), BF16)], mine, behind, ahead, low, high
    )[0]


def row_sums(blocks, first, weights, half, dtype):
    count, block = len(weights), blocks.shape[-1]
    units, width = weights[0].shape

    def row_sums_of(b_ref, *refs):
        w_refs, out_ref, held = refs[:count], refs[count], refs[count + 1]
        for c in range(2):
            for k in range(count):
                at = slice((first + k) * units, (first + k + 1) * units)
                held[k, c * block : (c + 1) * block] = b_ref[2 * half + c, at].T
        for p in range(width // WIDTH):
            at = slice(p * WIDTH, (p + 1) * WIDTH)
            total = jnp.dot(held[0], w_refs[0][:, at], preferred_element_type=F32)
            for k in range(1, count):
                total += jnp.dot(held[k], w_refs[k][:, at], preferred_element_type=F32)
            out_ref[:, at] = total.astype(dtype)

    return local(
        row_sums_of,
        [((2 * block, width), dtype)],
        blocks,
        *weights,
        scratch=[pltpu.VMEM((count, 2 * block, units), BF16)],
        flops=4 * count * block * units * width,
    )[0]


def merged(own, other):
    rows, width = own.shape
    each = rows // WAYS

    def merged_of(own_ref, other_ref, *out_refs):
        for k, out_ref in enumerate(out_refs):
            at = slice(k * each, (k + 1) * each)
            out_ref[...] = (own_ref[at] + other_ref[at].astype(F32)).astype(out_ref.dtype)

    return local(
        merged_of, [((each, width), F32 if k == 0 else BF16) for k in range(WAYS)], own, other
    )


def collected(outs, grads, peers):
    rows, width = outs[0].shape
    each = rows // peers

    def collected_of(*refs):
        def total(parts, at):
            value = parts[0][at]
            for part in parts[1:]:
                value = value + part[at].astype(F32)
            return value

        for p in range(0, peers, 2):
            at = slice(p * each, (p + 2) * each)
            out, grad = total(refs[:WAYS], at), total(refs[WAYS : 2 * WAYS], at)
            refs[-1][p] = jnp.concatenate([out[:each], grad[:each]]).astype(BF16)
            refs[-1][p + 1] = jnp.concatenate([out[each:], grad[each:]]).astype(BF16)

    return local(collected_of, [((peers, 2 * each, width), BF16)], *outs, *grads)[0]


def totals(parts):
    peers, rows, width = parts.shape

    def totals_of(parts_ref, out_ref, grad_ref):
        for at in range(0, width, WIDTH):
            columns = slice(at, at + WIDTH)
            total = parts_ref[0, :, columns].astype(F32)
            for p in range(1, peers):
                total += parts_ref[p, :, columns].astype(F32)
            out_ref[:, columns] = total[: rows // 2].astype(BF16)
            grad_ref[:, columns] = total[rows // 2 :].astype(BF16)

    return local(totals_of, [((rows // 2, width), BF16)] * 2, parts)


def weight_grads(blocks, own_t, other_t, own_g, other_g, factor):
    _, rows, block = blocks.shape
    units, width = rows // 3, own_t.shape[1]

    def weight_grads_of(b_ref, own_t, other_t, own_g, other_g, gate_ref, up_ref, down_ref, held):
        @pl.when(pl.program_id(0) == 0)
        def _():
            for c in range(WAYS):
                held[:, c * block : (c + 1) * block] = b_ref[c]

        for k, out_ref in enumerate((down_ref, gate_ref, up_ref)):
            own_ref, other_ref = (own_t, other_t) if k else (own_g, other_g)
            at = slice(k * units, (k + 1) * units)
            total = jnp.dot(held[at, : 2 * block], own_ref[...], preferred_element_type=F32)
            total += jnp.dot(held[at, 2 * block :], other_ref[...], preferred_element_type=F32)
            out_ref[...] = (total * factor).astype(BF16)

    token_rows = pl.BlockSpec((2 * block, WIDTH), lambda i: (0, i))
    columns = pl.BlockSpec((units, WIDTH), lambda i: (0, i))
    return pl.pallas_call(
        weight_grads_of,
        grid=(width // WIDTH,),
        in_specs=[VMEM] + [token_rows] * 4,
        out_specs=[columns] * 3,
        out_shape=[jax.ShapeDtypeStruct((units, width), BF16)] * 3,
        scratch_shapes=[pltpu.VMEM((rows, WAYS * block), BF16)],
        compiler_params=PARAMS,
        cost_estimate=pl.CostEstimate(
            flops=8 * block * rows * width, bytes_accessed=2 * rows * width, transcendentals=0
        ),
        name="weight_grads",
    )(blocks, own_t, other_t, own_g, other_g)


def per_device(tokens, gate_weight, up_weight, down_weight, out_grad):
    rows, width = tokens.shape
    factor = 1.0 / math.sqrt(rows * math.prod(lax.axis_size(axis) for axis in CUBE))

    peers = NEAR * lax.axis_size("gz")
    by_peer = first_exchange(copies(tokens, out_grad, peers))
    t_rows, g_rows = parted(by_peer)
    t_rows = [t_rows] + [turned(t_rows, k) for k in (1, 2, 3)]
    g_rows = [g_rows] + [turned(g_rows, k) for k in (1, 2, 3)]
    own_t = stacked(*t_rows)
    other_t = swapped(own_t)
    gate_up = gate_up_sums(own_t, other_t, gate_weight, up_weight)
    own_g = stacked(*g_rows)
    other_g = swapped(own_g)
    *sums, mine = ring_blocks(gate_up, own_g, other_g, down_weight)
    mine = activations(*ring_sums(*sums), mine)
    blocks = ring_gather(mine)

    out_theirs = row_sums(blocks, 0, (down_weight,), 1, BF16)
    grad_theirs = row_sums(after(blocks, out_theirs), 1, (gate_weight, up_weight), 1, BF16)
    out_ours = row_sums(after(blocks, grad_theirs), 0, (down_weight,), 0, F32)
    grad_ours = row_sums(after(blocks, out_ours), 1, (gate_weight, up_weight), 0, F32)
    outs = merged(after(out_ours, grad_ours), swapped(out_theirs))
    outs = [outs[0]] + [turned(outs[k], -k) for k in (1, 2, 3)]
    grads = merged(grad_ours, swapped(grad_theirs))
    rows_all = after((own_t, other_t, own_g, other_g), grads)
    grads = [grads[0]] + [turned(grads[k], -k) for k in (1, 2, 3)]
    gate_grad, up_grad, down_grad = weight_grads(blocks, *rows_all, factor)
    outs[0] = after(outs[0], gate_grad)
    parts = first_exchange(collected(outs, grads, peers))
    output, tokens_grad = totals(parts)
    return output, tokens_grad, gate_grad, up_grad, down_grad


def solution(mesh):
    placed = P(("dcn", "gx", "gz"), "gy")
    return jax.shard_map(
        per_device,
        mesh=mesh,
        in_specs=(placed,) * 5,
        out_specs=(placed,) * 5,
        check_vma=False,
    )
```

```python
import math

import jax
import jax.numpy as jnp
from jax import lax
from jax.experimental import pallas as pl
from jax.experimental.pallas import tpu as pltpu
from jax.sharding import PartitionSpec as P

BF16, F32 = jnp.bfloat16, jnp.float32
CUBE = ("dcn", "gx", "gz")
NEAR = 2
WIDTH = 512
WAYS = 4
SMEM = pl.BlockSpec(memory_space=pltpu.SMEM)
VMEM = pl.BlockSpec(memory_space=pltpu.VMEM)
PARAMS = pltpu.CompilerParams(vmem_limit_bytes=24 * 1024 * 1024)


def local(kernel, out_shape, *args, scratch=(), flops=1e6, moved=1e6):
    return pl.pallas_call(
        kernel,
        in_specs=[SMEM if a.dtype == jnp.int32 else VMEM for a in args],
        out_specs=[VMEM] * len(out_shape),
        out_shape=[jax.ShapeDtypeStruct(*s) for s in out_shape],
        scratch_shapes=list(scratch),
        compiler_params=PARAMS,
        cost_estimate=pl.CostEstimate(flops=int(flops), bytes_accessed=int(moved), transcendentals=0),
        name=kernel.__name__,
    )(*args)


def swapped(x):
    return lax.ppermute(x, "dcn", [(0, 1), (1, 0)])


def after(x, *others):
    return lax.optimization_barrier((x, *others))[0]


def copies(tokens, out_grad, peers):
    rows, width = tokens.shape

    def copies_of(t_hbm, g_hbm, out_ref, t_ref, g_ref, sems):
        moves = [
            pltpu.make_async_copy(t_hbm, t_ref, sems.at[0]),
            pltpu.make_async_copy(g_hbm, g_ref, sems.at[1]),
        ]
        for move in moves:
            move.start()
        for move in moves:
            move.wait()
        both = jnp.concatenate([t_ref[...].astype(F32), g_ref[...].astype(F32)]).astype(BF16)
        for p in range(peers):
            out_ref[p] = both

    in_hbm = pl.BlockSpec(memory_space=pltpu.HBM)
    return pl.pallas_call(
        copies_of,
        in_specs=[in_hbm] * 2,
        out_specs=VMEM,
        out_shape=jax.ShapeDtypeStruct((peers, 2 * rows, width), BF16),
        scratch_shapes=[pltpu.VMEM((rows, width), BF16)] * 2 + [pltpu.SemaphoreType.DMA((2,))],
        compiler_params=PARAMS,
        name="copies",
    )(*(pltpu.with_memory_space_constraint(x, pltpu.HBM) for x in (tokens, out_grad)))


def parted(rows_of_peers):
    peers, rows, width = rows_of_peers.shape
    half = rows // 2

    def parted_of(in_ref, t_ref, g_ref):
        for p in range(0, peers, 2):
            first, second = in_ref[p].astype(F32), in_ref[p + 1].astype(F32)
            to = slice(p * half, (p + 2) * half)
            t_ref[to] = jnp.concatenate([first[:half], second[:half]]).astype(BF16)
            g_ref[to] = jnp.concatenate([first[half:], second[half:]]).astype(BF16)

    return local(parted_of, [((peers * half, width), BF16)] * 2, rows_of_peers)


def stacked(*blocks):
    rows, width = blocks[0].shape

    def stacked_of(*refs):
        for k, ref in enumerate(refs[:-1]):
            refs[-1][k * rows : (k + 1) * rows] = ref[...]

    return local(stacked_of, [((len(blocks) * rows, width), BF16)], *blocks)[0]


def sums_into(held, first, w_ref, own_ref, other_ref):
    units, block = w_ref.shape[0], held.shape[-1]
    for half, rows_ref in enumerate((own_ref, other_ref)):
        sums = lax.dot_general(
            w_ref[...], rows_ref[...], (((1,), (1,)), ((), ())), preferred_element_type=F32
        )
        for c in range(2):
            held[2 * half + c, first : first + units] = sums[:, c * block : (c + 1) * block]


def ring_blocks(own, other, weights):
    count = len(weights)
    units, width = weights[0].shape
    rows = own.shape[0]
    block, part = rows // 2, count * units // 2

    def ring_blocks_of(own_ref, other_ref, *refs):
        w_refs = refs[:count]
        forth, back, next_, before, mine, held = refs[count:]
        for k, w_ref in enumerate(w_refs):
            sums_into(held, k * units, w_ref, own_ref, other_ref)
        me = lax.axis_index("gy")
        after_, far, last = (lax.rem(me + s, WAYS) for s in (1, 2, 3))
        forth[:part] = held[far, :part].astype(BF16)
        forth[part:] = held[after_, part:].astype(BF16)
        back[:part] = held[far, part:].astype(BF16)
        back[part:] = held[last, :part].astype(BF16)
        next_[...] = held[after_, :part]
        before[...] = held[last, part:]
        mine[...] = held[me]

    full = (2 * part, block)
    return local(
        ring_blocks_of,
        [(full, BF16)] * 2 + [((part, block), F32)] * 2 + [(full, F32)],
        own,
        other,
        *weights,
        scratch=[pltpu.VMEM((WAYS,) + full, F32)],
        flops=4 * count * units * width * rows,
    )


def shifted(x, by):
    n = lax.axis_size("gy")
    return lax.ppermute(x, "gy", [(i, (i + by) % n) for i in range(n)])


def plane():
    cores, ys, zs = lax.axis_size("dcn"), lax.axis_size("gx") // NEAR, lax.axis_size("gz")
    return cores, ys, zs, lambda d, n, y, z: ((d * NEAR + n) * ys + y) * zs + z


def first_groups():
    cores, ys, zs, place = plane()
    by_z = [[place(0, n, y, z) for n in range(NEAR) for z in range(zs)] for y in range(ys)]
    by_y = [[place(1, n, y, z) for n in range(NEAR) for y in range(ys)] for z in range(zs)]
    return by_z + by_y


def first_exchange(x):
    return lax.all_to_all(x, CUBE, 0, 0, axis_index_groups=first_groups(), tiled=True)


def turned(x, by_even, by_odd):
    cores, ys, zs, place = plane()
    ways = lax.axis_size("gy")
    pairs = []
    for n in range(NEAR):
        for y in range(ys):
            for z in range(zs):
                for g in range(ways):
                    by = by_odd if g % 2 else by_even
                    for d, to in ((0, ((y + by) % ys, z)), (1, (y, (z + by) % zs))):
                        places = place(d, n, y, z), place(d, n, *to)
                        pairs.append(tuple((p // zs * ways + g) * zs + p % zs for p in places))
    return lax.ppermute(x, ("dcn", "gx", "gy", "gz"), pairs)


def joined(here, there):
    part, block = here.shape

    def joined_of(here_ref, there_ref, out_ref):
        out_ref[...] = (here_ref[...] + there_ref[:part].astype(F32)).astype(BF16)

    return local(joined_of, [((part, block), BF16)], here, there)[0]


def block_sum(out, behind_ref, ahead_ref, low_ref, high_ref, mine_ref):
    part = low_ref.shape[0]
    out[:part] = mine_ref[:part] + low_ref[...].astype(F32) + ahead_ref[part:].astype(F32)
    out[part:] = mine_ref[part:] + high_ref[...].astype(F32) + behind_ref[part:].astype(F32)


def activations(*parts):
    rows, block = parts[-1].shape
    units = rows // 2

    def activations_of(behind, ahead, low, high, mine, hidden_ref, gate_ref, up_ref, total):
        block_sum(total, behind, ahead, low, high, mine)
        gate, up = total[:units], total[units:]
        sigmoid = jax.nn.sigmoid(gate)
        hidden_ref[...] = (gate * sigmoid * up).astype(BF16)
        gate_ref[...] = up * sigmoid * (1.0 + gate * (1.0 - sigmoid))
        up_ref[...] = gate * sigmoid

    one = ((units, block), F32)
    return local(
        activations_of,
        [((units, block), BF16), one, one],
        *parts,
        scratch=[pltpu.VMEM((rows, block), F32)],
    )


def deltas_from(hidden, gate_factor, up_factor, *parts):
    units, block = parts[-1].shape

    def deltas_of(hidden_ref, gate_ref, up_ref, behind, ahead, low, high, mine, out_ref, total):
        block_sum(total, behind, ahead, low, high, mine)
        out_ref[:units] = hidden_ref[...]
        out_ref[units : 2 * units] = (total[...] * gate_ref[...]).astype(BF16)
        out_ref[2 * units :] = (total[...] * up_ref[...]).astype(BF16)

    return local(
        deltas_of,
        [((3 * units, block), BF16)],
        hidden,
        gate_factor,
        up_factor,
        *parts,
        scratch=[pltpu.VMEM((units, block), F32)],
    )[0]


def placed(mine, behind, ahead, low, high):
    rows, block = mine.shape
    part = rows // 2

    def placed_of(mine_ref, behind_ref, ahead_ref, low_ref, high_ref, out_ref):
        me = lax.axis_index("gy")
        far = lax.rem(me + 2, WAYS)
        out_ref[me] = mine_ref[...]
        out_ref[lax.rem(me + 3, WAYS)] = behind_ref[...]
        out_ref[lax.rem(me + 1, WAYS)] = ahead_ref[...]
        out_ref[far, :part] = low_ref[...]
        out_ref[far, part:] = high_ref[...]

    return local(placed_of, [((WAYS, rows, block), BF16)], mine, behind, ahead, low, high)[0]


def both_ways(forth, back):
    return shifted(forth, 1), shifted(back, -1)


def early_chunk(me):
    return 3 - lax.rem(me, 2)


def rows_into(held, blocks, w_refs, store):
    gate, up, down = w_refs
    units, width = down.shape
    block = blocks[0].shape[-1]
    for k, ref in enumerate(blocks):
        for which in range(3):
            held[which, k * block : (k + 1) * block] = ref[which * units : (which + 1) * units].T
    for p in range(width // WIDTH):
        at = slice(p * WIDTH, (p + 1) * WIDTH)
        dot = lambda which, w: jnp.dot(held[which], w[:, at], preferred_element_type=F32)
        store(0, at, dot(0, down))
        store(1, at, dot(1, gate) + dot(2, up))


def near_rows(mine, behind, ahead, weights):
    rows, block = mine.shape
    units, width = weights[0].shape

    def near_rows_of(m_ref, b_ref, a_ref, w0, w1, w2, rows_ref, early_ref, held):
        me = lax.axis_index("gy")
        slots = [lax.rem(me + s, WAYS) for s in (0, 3, 1)]

        def store(kind, at, total):
            for k, slot in enumerate(slots):
                rows_ref[slot, kind, :, at] = total[k * block : (k + 1) * block]

        rows_into(held, (m_ref, b_ref, a_ref), (w0, w1, w2), store)
        early_ref[...] = rows_ref[early_chunk(me)].astype(BF16)

    return local(
        near_rows_of,
        [((WAYS, 2, block, width), F32), ((2, block, width), BF16)],
        mine,
        behind,
        ahead,
        *weights,
        scratch=[pltpu.VMEM((3, 3 * block, units), BF16)],
        flops=18 * block * units * width,
    )


def far_rows(low, high, weights, near):
    part, block = low.shape
    units, width = weights[0].shape

    def far_rows_of(low_ref, high_ref, w0, w1, w2, near_ref, rows_ref, late_ref, held, far_block):
        me = lax.axis_index("gy")
        far_block[:part] = low_ref[...]
        far_block[part:] = high_ref[...]

        def store(kind, at, total):
            rows_ref[kind, :, at] = total

        rows_into(held, (far_block,), (w0, w1, w2), store)

        @pl.when(me < 2)
        def _():
            late_ref[...] = rows_ref[...].astype(BF16)

        @pl.when(me >= 2)
        def _():
            late_ref[...] = near_ref[me].astype(BF16)

    return local(
        far_rows_of,
        [((2, block, width), F32), ((2, block, width), BF16)],
        low,
        high,
        *weights,
        near,
        scratch=[pltpu.VMEM((3, block, units), BF16), pltpu.VMEM((2 * part, block), BF16)],
        flops=6 * block * units * width,
    )


def early_quarter(near, early):
    _, _, block, width = near.shape
    each = 2 * block // WAYS

    def early_quarter_of(near_ref, early_ref, out_ref):
        me = lax.axis_index("gy")
        odd = lax.rem(me, 2)
        at = pl.ds(pl.multiple_of(odd * each, each), each)
        for kind in range(2):
            own = near_ref[early_chunk(me) - 2, kind, at]
            out_ref[kind] = (own + early_ref[kind, at].astype(F32)).astype(BF16)

    return local(early_quarter_of, [((2, each, width), BF16)], near, early)[0]


def late_quarters(near, far, early, late):
    _, _, block, width = near.shape
    each = 2 * block // WAYS

    def late_quarters_of(near_ref, far_ref, early_ref, late_ref, mine_ref, *out_refs):
        me = lax.axis_index("gy")
        odd = lax.rem(me, 2)

        def quarter(k, kind):
            chunk, first = k * each // block, k * each % block
            at = slice(first, first + each)
            is_far, is_early = lax.rem(me + 2, WAYS) == chunk, early_chunk(me) == chunk + 2
            own = jnp.where(is_far, far_ref[kind, at], near_ref[chunk, kind, at])
            other = jnp.where(is_early, early_ref[kind, at], late_ref[kind, at])
            return own + other.astype(F32)

        for kind in range(2):
            mine_ref[kind] = quarter(0, kind)

        @pl.when(odd == 1)
        def _():
            for kind in range(2):
                for out_ref, k in zip(out_refs, (2, 3)):
                    out_ref[kind] = quarter(k, kind).astype(BF16)

        @pl.when(odd == 0)
        def _():
            for kind in range(2):
                for out_ref, k in zip(out_refs, (3, 1)):
                    out_ref[kind] = quarter(k, kind).astype(BF16)

    shape = (2, each, width)
    return local(
        late_quarters_of,
        [(shape, F32), (shape, BF16), (shape, BF16)],
        near,
        far,
        early,
        late,
    )


def collected(parts, peers):
    _, rows, width = parts[0].shape
    each = rows // peers

    def collected_of(*refs):
        for p in range(0, peers, 2):
            at = slice(p * each, (p + 2) * each)
            out, grad = refs[0][0, at], refs[0][1, at]
            for ref in refs[1:WAYS]:
                out, grad = out + ref[0, at].astype(F32), grad + ref[1, at].astype(F32)
            refs[-1][p] = jnp.concatenate([out[:each], grad[:each]]).astype(BF16)
            refs[-1][p + 1] = jnp.concatenate([out[each:], grad[each:]]).astype(BF16)

    return local(collected_of, [((peers, 2 * each, width), BF16)], *parts)[0]


def totals(parts):
    peers, rows, width = parts.shape

    def totals_of(parts_ref, out_ref, grad_ref):
        for at in range(0, width, WIDTH):
            columns = slice(at, at + WIDTH)
            total = parts_ref[0, :, columns].astype(F32)
            for p in range(1, peers):
                total += parts_ref[p, :, columns].astype(F32)
            out_ref[:, columns] = total[: rows // 2].astype(BF16)
            grad_ref[:, columns] = total[rows // 2 :].astype(BF16)

    return local(totals_of, [((rows // 2, width), BF16)] * 2, parts)


def weight_grads(blocks, own_t, other_t, own_g, other_g, factor):
    _, rows, block = blocks.shape
    units, width = rows // 3, own_t.shape[1]

    def weight_grads_of(b_ref, own_t, other_t, own_g, other_g, gate_ref, up_ref, down_ref, held):
        @pl.when(pl.program_id(0) == 0)
        def _():
            for c in range(WAYS):
                held[:, c * block : (c + 1) * block] = b_ref[c]

        for k, out_ref in enumerate((down_ref, gate_ref, up_ref)):
            own_ref, other_ref = (own_t, other_t) if k else (own_g, other_g)
            at = slice(k * units, (k + 1) * units)
            total = jnp.dot(held[at, : 2 * block], own_ref[...], preferred_element_type=F32)
            total += jnp.dot(held[at, 2 * block :], other_ref[...], preferred_element_type=F32)
            out_ref[...] = (total * factor).astype(BF16)

    token_rows = pl.BlockSpec((2 * block, WIDTH), lambda i: (0, i))
    columns = pl.BlockSpec((units, WIDTH), lambda i: (0, i))
    return pl.pallas_call(
        weight_grads_of,
        grid=(width // WIDTH,),
        in_specs=[VMEM] + [token_rows] * 4,
        out_specs=[columns] * 3,
        out_shape=[jax.ShapeDtypeStruct((units, width), BF16)] * 3,
        scratch_shapes=[pltpu.VMEM((rows, WAYS * block), BF16)],
        compiler_params=PARAMS,
        cost_estimate=pl.CostEstimate(
            flops=8 * block * rows * width, bytes_accessed=2 * rows * width, transcendentals=0
        ),
        name="weight_grads",
    )(blocks, own_t, other_t, own_g, other_g)


def per_device(tokens, gate_weight, up_weight, down_weight, out_grad):
    rows, width = tokens.shape
    factor = 1.0 / math.sqrt(rows * math.prod(lax.axis_size(axis) for axis in CUBE))

    peers = NEAR * lax.axis_size("gz")
    by_peer = first_exchange(copies(tokens, out_grad, peers))
    t_rows, g_rows = parted(by_peer)
    t_rows = [t_rows] + [turned(t_rows, k, k) for k in (1, 2, 3)]
    g_rows = [g_rows] + [turned(g_rows, k, k) for k in (1, 2, 3)]
    own_t, own_g = stacked(*t_rows), stacked(*g_rows)
    other_t = swapped(own_t)
    *gate_up, gate_up_mine = ring_blocks(own_t, other_t, (gate_weight, up_weight))
    other_g = swapped(own_g)
    *hgrad, hgrad_mine = ring_blocks(own_g, other_g, (down_weight,))

    near = both_ways(*gate_up[:2])
    hgrad_near = both_ways(*hgrad[:2])
    gate_up[2], gate_up[3] = after((gate_up[2], gate_up[3]), hgrad)
    low = joined(gate_up[2], near[0])
    high = joined(gate_up[3], near[1])
    far = both_ways(low, high)
    hgrad_low = joined(after(hgrad[2], low, high), hgrad_near[0])
    hgrad_high = joined(after(hgrad[3], low, high), hgrad_near[1])
    hgrad_far = both_ways(hgrad_low, hgrad_high)
    gate_up_mine = after(gate_up_mine, hgrad_low, hgrad_high)
    hidden, *factors = activations(*near, *far, gate_up_mine)
    blocks = deltas_from(hidden, *factors, *hgrad_near, *hgrad_far, hgrad_mine)
    weights = (gate_weight, up_weight, down_weight)
    mine = blocks
    behind, ahead = both_ways(mine, mine)
    part = mine.shape[0] // 2
    far = both_ways(behind[:part], ahead[part:])
    near, early = near_rows(mine, behind, ahead, weights)
    early = swapped(early)
    first = turned(early_quarter(near, early), -2, -1)
    far_own, late = far_rows(*far, weights, near)
    sums = late_quarters(near, far_own, early, swapped(late))
    blocks = placed(after(mine, sums), behind, ahead, *far)
    sums = [sums[0], first, turned(sums[1], -3, -2), turned(sums[2], -1, -3)]
    gate_grad, up_grad, down_grad = weight_grads(blocks, own_t, other_t, own_g, other_g, factor)
    sums[0] = after(sums[0], gate_grad)
    parts = first_exchange(collected(sums, peers))
    output, tokens_grad = totals(parts)
    return output, tokens_grad, gate_grad, up_grad, down_grad


def solution(mesh):
    placed = P(("dcn", "gx", "gz"), "gy")
    return jax.shard_map(
        per_device,
        mesh=mesh,
        in_specs=(placed,) * 5,
        out_specs=(placed,) * 5,
        check_vma=False,
    )
```

```python
import math

import jax
import jax.numpy as jnp
from jax import lax
from jax.experimental import pallas as pl
from jax.experimental.pallas import tpu as pltpu
from jax.sharding import PartitionSpec as P

BF16, F32 = jnp.bfloat16, jnp.float32
CUBE = ("dcn", "gx", "gz")
NEAR = 2
WIDTH = 512
WAYS = 4
SMEM = pl.BlockSpec(memory_space=pltpu.SMEM)
VMEM = pl.BlockSpec(memory_space=pltpu.VMEM)
PARAMS = pltpu.CompilerParams(vmem_limit_bytes=24 * 1024 * 1024)


def local(kernel, out_shape, *args, scratch=(), flops=1e6, moved=1e6):
    return pl.pallas_call(
        kernel,
        in_specs=[SMEM if a.dtype == jnp.int32 else VMEM for a in args],
        out_specs=[VMEM] * len(out_shape),
        out_shape=[jax.ShapeDtypeStruct(*s) for s in out_shape],
        scratch_shapes=list(scratch),
        compiler_params=PARAMS,
        cost_estimate=pl.CostEstimate(flops=int(flops), bytes_accessed=int(moved), transcendentals=0),
        name=kernel.__name__,
    )(*args)


def swapped(x):
    return lax.ppermute(x, "dcn", [(0, 1), (1, 0)])


def after(x, *others):
    return lax.optimization_barrier((x, *others))[0]


def copies(tokens, out_grad, peers):
    rows, width = tokens.shape

    def copies_of(t_hbm, g_hbm, out_ref, t_ref, g_ref, sems):
        moves = [
            pltpu.make_async_copy(t_hbm, t_ref, sems.at[0]),
            pltpu.make_async_copy(g_hbm, g_ref, sems.at[1]),
        ]
        for move in moves:
            move.start()
        for move in moves:
            move.wait()
        both = jnp.concatenate([t_ref[...].astype(F32), g_ref[...].astype(F32)]).astype(BF16)
        for p in range(peers):
            out_ref[p] = both

    in_hbm = pl.BlockSpec(memory_space=pltpu.HBM)
    return pl.pallas_call(
        copies_of,
        in_specs=[in_hbm] * 2,
        out_specs=VMEM,
        out_shape=jax.ShapeDtypeStruct((peers, 2 * rows, width), BF16),
        scratch_shapes=[pltpu.VMEM((rows, width), BF16)] * 2 + [pltpu.SemaphoreType.DMA((2,))],
        compiler_params=PARAMS,
        name="copies",
    )(*(pltpu.with_memory_space_constraint(x, pltpu.HBM) for x in (tokens, out_grad)))


def parted(rows_of_peers):
    peers, rows, width = rows_of_peers.shape
    half = rows // 2

    def parted_of(in_ref, t_ref, g_ref):
        for p in range(0, peers, 2):
            first, second = in_ref[p].astype(F32), in_ref[p + 1].astype(F32)
            to = slice(p * half, (p + 2) * half)
            t_ref[to] = jnp.concatenate([first[:half], second[:half]]).astype(BF16)
            g_ref[to] = jnp.concatenate([first[half:], second[half:]]).astype(BF16)

    return local(parted_of, [((peers * half, width), BF16)] * 2, rows_of_peers)


def stacked(*blocks):
    rows, width = blocks[0].shape

    def stacked_of(*refs):
        for k, ref in enumerate(refs[:-1]):
            refs[-1][k * rows : (k + 1) * rows] = ref[...]

    return local(stacked_of, [((len(blocks) * rows, width), BF16)], *blocks)[0]


def sums_into(held, first, w_ref, own_ref, other_ref):
    units, block = w_ref.shape[0], held.shape[-1]
    for half, rows_ref in enumerate((own_ref, other_ref)):
        sums = lax.dot_general(
            w_ref[...], rows_ref[...], (((1,), (1,)), ((), ())), preferred_element_type=F32
        )
        for c in range(2):
            held[2 * half + c, first : first + units] = sums[:, c * block : (c + 1) * block]


def ring_blocks(own, other, weights):
    count = len(weights)
    units, width = weights[0].shape
    rows = own.shape[0]
    block, part = rows // 2, count * units // 2

    def ring_blocks_of(own_ref, other_ref, *refs):
        w_refs = refs[:count]
        forth, back, next_, before, mine, held = refs[count:]
        for k, w_ref in enumerate(w_refs):
            sums_into(held, k * units, w_ref, own_ref, other_ref)
        me = lax.axis_index("gy")
        after_, far, last = (lax.rem(me + s, WAYS) for s in (1, 2, 3))
        forth[:part] = held[far, :part].astype(BF16)
        forth[part:] = held[after_, part:].astype(BF16)
        back[:part] = held[far, part:].astype(BF16)
        back[part:] = held[last, :part].astype(BF16)
        next_[...] = held[after_, :part]
        before[...] = held[last, part:]
        mine[...] = held[me]

    full = (2 * part, block)
    return local(
        ring_blocks_of,
        [(full, BF16)] * 2 + [((part, block), F32)] * 2 + [(full, F32)],
        own,
        other,
        *weights,
        scratch=[pltpu.VMEM((WAYS,) + full, F32)],
        flops=4 * count * units * width * rows,
    )


def shifted(x, by):
    n = lax.axis_size("gy")
    return lax.ppermute(x, "gy", [(i, (i + by) % n) for i in range(n)])


def plane():
    cores, ys, zs = lax.axis_size("dcn"), lax.axis_size("gx") // NEAR, lax.axis_size("gz")
    return cores, ys, zs, lambda d, n, y, z: ((d * NEAR + n) * ys + y) * zs + z


def first_groups():
    cores, ys, zs, place = plane()
    by_z = [[place(0, n, y, z) for n in range(NEAR) for z in range(zs)] for y in range(ys)]
    by_y = [[place(1, n, y, z) for n in range(NEAR) for y in range(ys)] for z in range(zs)]
    return by_z + by_y


def first_exchange(x):
    return lax.all_to_all(x, CUBE, 0, 0, axis_index_groups=first_groups(), tiled=True)


def turned(x, by_even, by_odd):
    cores, ys, zs, place = plane()
    ways = lax.axis_size("gy")
    pairs = []
    for n in range(NEAR):
        for y in range(ys):
            for z in range(zs):
                for g in range(ways):
                    by = by_odd if g % 2 else by_even
                    for d, to in ((0, ((y + by) % ys, z)), (1, (y, (z + by) % zs))):
                        places = place(d, n, y, z), place(d, n, *to)
                        pairs.append(tuple((p // zs * ways + g) * zs + p % zs for p in places))
    return lax.ppermute(x, ("dcn", "gx", "gy", "gz"), pairs)


def joined(here, there):
    part, block = here.shape

    def joined_of(here_ref, there_ref, out_ref):
        out_ref[...] = (here_ref[...] + there_ref[:part].astype(F32)).astype(BF16)

    return local(joined_of, [((part, block), BF16)], here, there)[0]


def block_sum(out, behind_ref, ahead_ref, low_ref, high_ref, mine_ref):
    part = low_ref.shape[0]
    out[:part] = mine_ref[:part] + low_ref[...].astype(F32) + ahead_ref[part:].astype(F32)
    out[part:] = mine_ref[part:] + high_ref[...].astype(F32) + behind_ref[part:].astype(F32)


def activations(*parts):
    rows, block = parts[-1].shape
    units = rows // 2

    def activations_of(behind, ahead, low, high, mine, hidden_ref, gate_ref, up_ref, total):
        block_sum(total, behind, ahead, low, high, mine)
        gate, up = total[:units], total[units:]
        sigmoid = jax.nn.sigmoid(gate)
        hidden_ref[...] = (gate * sigmoid * up).astype(BF16)
        gate_ref[...] = up * sigmoid * (1.0 + gate * (1.0 - sigmoid))
        up_ref[...] = gate * sigmoid

    one = ((units, block), F32)
    return local(
        activations_of,
        [((units, block), BF16), one, one],
        *parts,
        scratch=[pltpu.VMEM((rows, block), F32)],
    )


def deltas_from(hidden, gate_factor, up_factor, *parts):
    units, block = parts[-1].shape

    def deltas_of(hidden_ref, gate_ref, up_ref, behind, ahead, low, high, mine, low_out, high_out, total):
        block_sum(total, behind, ahead, low, high, mine)
        rest = units // 2
        gate = (total[...] * gate_ref[...]).astype(BF16)
        low_out[:units] = hidden_ref[...]
        low_out[units:] = gate[:rest]
        high_out[:rest] = gate[rest:]
        high_out[rest:] = (total[...] * up_ref[...]).astype(BF16)

    return local(
        deltas_of,
        [((3 * units // 2, block), BF16)] * 2,
        hidden,
        gate_factor,
        up_factor,
        *parts,
        scratch=[pltpu.VMEM((units, block), F32)],
    )


def placed(*halves):
    part, block = halves[0].shape

    def placed_of(*refs):
        me, out_ref = lax.axis_index("gy"), refs[-1]
        for k, step in enumerate((0, 3, 1, 2)):
            slot = lax.rem(me + step, WAYS)
            out_ref[slot, :part] = refs[2 * k][...]
            out_ref[slot, part:] = refs[2 * k + 1][...]

    return local(placed_of, [((WAYS, 2 * part, block), BF16)], *halves)[0]


def both_ways(forth, back):
    return shifted(forth, 1), shifted(back, -1)


def early_chunk(me):
    return 3 - lax.rem(me, 2)


def rows_into(held, blocks, w_refs, store):
    gate, up, down = w_refs
    units, width = down.shape
    block = blocks[0].shape[-1]
    for k, ref in enumerate(blocks):
        for which in range(3):
            held[which, k * block : (k + 1) * block] = ref[which * units : (which + 1) * units].T
    for p in range(width // WIDTH):
        at = slice(p * WIDTH, (p + 1) * WIDTH)
        dot = lambda which, w: jnp.dot(held[which], w[:, at], preferred_element_type=F32)
        store(0, at, dot(0, down))
        store(1, at, dot(1, gate) + dot(2, up))


def near_rows(halves, weights):
    part, block = halves[0].shape
    units, width = weights[0].shape

    def near_rows_of(*refs):
        (w0, w1, w2, rows_ref, early_ref, held, *whole), halves_of = refs[6:], refs[:6]
        for k, ref in enumerate(whole):
            ref[:part] = halves_of[2 * k][...]
            ref[part:] = halves_of[2 * k + 1][...]
        me = lax.axis_index("gy")
        slots = [lax.rem(me + s, WAYS) for s in (0, 3, 1)]

        def store(kind, at, total):
            for k, slot in enumerate(slots):
                rows_ref[slot, kind, :, at] = total[k * block : (k + 1) * block]

        rows_into(held, whole, (w0, w1, w2), store)
        early_ref[...] = rows_ref[early_chunk(me)].astype(BF16)

    return local(
        near_rows_of,
        [((WAYS, 2, block, width), F32), ((2, block, width), BF16)],
        *halves,
        *weights,
        scratch=[pltpu.VMEM((3, 3 * block, units), BF16)] + [pltpu.VMEM((2 * part, block), BF16)] * 3,
        flops=18 * block * units * width,
    )


def far_rows(low, high, weights, near):
    part, block = low.shape
    units, width = weights[0].shape

    def far_rows_of(low_ref, high_ref, w0, w1, w2, near_ref, rows_ref, late_ref, held, far_block):
        me = lax.axis_index("gy")
        far_block[:part] = low_ref[...]
        far_block[part:] = high_ref[...]

        def store(kind, at, total):
            rows_ref[kind, :, at] = total

        rows_into(held, (far_block,), (w0, w1, w2), store)

        @pl.when(me < 2)
        def _():
            late_ref[...] = rows_ref[...].astype(BF16)

        @pl.when(me >= 2)
        def _():
            late_ref[...] = near_ref[me].astype(BF16)

    return local(
        far_rows_of,
        [((2, block, width), F32), ((2, block, width), BF16)],
        low,
        high,
        *weights,
        near,
        scratch=[pltpu.VMEM((3, block, units), BF16), pltpu.VMEM((2 * part, block), BF16)],
        flops=6 * block * units * width,
    )


def early_quarter(near, early):
    _, _, block, width = near.shape
    each = 2 * block // WAYS

    def early_quarter_of(near_ref, early_ref, out_ref):
        me = lax.axis_index("gy")
        odd = lax.rem(me, 2)
        at = pl.ds(pl.multiple_of(odd * each, each), each)
        for kind in range(2):
            own = near_ref[early_chunk(me) - 2, kind, at]
            out_ref[kind] = (own + early_ref[kind, at].astype(F32)).astype(BF16)

    return local(early_quarter_of, [((2, each, width), BF16)], near, early)[0]


def late_quarters(near, far, early, late):
    _, _, block, width = near.shape
    each = 2 * block // WAYS

    def late_quarters_of(near_ref, far_ref, early_ref, late_ref, mine_ref, *out_refs):
        me = lax.axis_index("gy")
        odd = lax.rem(me, 2)

        def quarter(k, kind):
            chunk, first = k * each // block, k * each % block
            at = slice(first, first + each)
            is_far, is_early = lax.rem(me + 2, WAYS) == chunk, early_chunk(me) == chunk + 2
            own = jnp.where(is_far, far_ref[kind, at], near_ref[chunk, kind, at])
            other = jnp.where(is_early, early_ref[kind, at], late_ref[kind, at])
            return own + other.astype(F32)

        for kind in range(2):
            mine_ref[kind] = quarter(0, kind)

        @pl.when(odd == 1)
        def _():
            for kind in range(2):
                for out_ref, k in zip(out_refs, (2, 3)):
                    out_ref[kind] = quarter(k, kind).astype(BF16)

        @pl.when(odd == 0)
        def _():
            for kind in range(2):
                for out_ref, k in zip(out_refs, (3, 1)):
                    out_ref[kind] = quarter(k, kind).astype(BF16)

    shape = (2, each, width)
    return local(
        late_quarters_of,
        [(shape, F32), (shape, BF16), (shape, BF16)],
        near,
        far,
        early,
        late,
    )


def collected(parts, peers):
    _, rows, width = parts[0].shape
    each = rows // peers

    def collected_of(*refs):
        for p in range(0, peers, 2):
            at = slice(p * each, (p + 2) * each)
            out, grad = refs[0][0, at], refs[0][1, at]
            for ref in refs[1:WAYS]:
                out, grad = out + ref[0, at].astype(F32), grad + ref[1, at].astype(F32)
            refs[-1][p] = jnp.concatenate([out[:each], grad[:each]]).astype(BF16)
            refs[-1][p + 1] = jnp.concatenate([out[each:], grad[each:]]).astype(BF16)

    return local(collected_of, [((peers, 2 * each, width), BF16)], *parts)[0]


def totals(parts):
    peers, rows, width = parts.shape

    def totals_of(parts_ref, out_ref, grad_ref):
        for at in range(0, width, WIDTH):
            columns = slice(at, at + WIDTH)
            total = parts_ref[0, :, columns].astype(F32)
            for p in range(1, peers):
                total += parts_ref[p, :, columns].astype(F32)
            out_ref[:, columns] = total[: rows // 2].astype(BF16)
            grad_ref[:, columns] = total[rows // 2 :].astype(BF16)

    return local(totals_of, [((rows // 2, width), BF16)] * 2, parts)


def weight_grads(blocks, own_t, other_t, own_g, other_g, factor):
    _, rows, block = blocks.shape
    units, width = rows // 3, own_t.shape[1]

    def weight_grads_of(b_ref, own_t, other_t, own_g, other_g, gate_ref, up_ref, down_ref, held):
        @pl.when(pl.program_id(0) == 0)
        def _():
            for c in range(WAYS):
                held[:, c * block : (c + 1) * block] = b_ref[c]

        for k, out_ref in enumerate((down_ref, gate_ref, up_ref)):
            own_ref, other_ref = (own_t, other_t) if k else (own_g, other_g)
            at = slice(k * units, (k + 1) * units)
            total = jnp.dot(held[at, : 2 * block], own_ref[...], preferred_element_type=F32)
            total += jnp.dot(held[at, 2 * block :], other_ref[...], preferred_element_type=F32)
            out_ref[...] = (total * factor).astype(BF16)

    token_rows = pl.BlockSpec((2 * block, WIDTH), lambda i: (0, i))
    columns = pl.BlockSpec((units, WIDTH), lambda i: (0, i))
    return pl.pallas_call(
        weight_grads_of,
        grid=(width // WIDTH,),
        in_specs=[VMEM] + [token_rows] * 4,
        out_specs=[columns] * 3,
        out_shape=[jax.ShapeDtypeStruct((units, width), BF16)] * 3,
        scratch_shapes=[pltpu.VMEM((rows, WAYS * block), BF16)],
        compiler_params=PARAMS,
        cost_estimate=pl.CostEstimate(
            flops=8 * block * rows * width, bytes_accessed=2 * rows * width, transcendentals=0
        ),
        name="weight_grads",
    )(blocks, own_t, other_t, own_g, other_g)


def per_device(tokens, gate_weight, up_weight, down_weight, out_grad):
    rows, width = tokens.shape
    factor = 1.0 / math.sqrt(rows * math.prod(lax.axis_size(axis) for axis in CUBE))

    peers = NEAR * lax.axis_size("gz")
    by_peer = first_exchange(copies(tokens, out_grad, peers))
    t_rows, g_rows = parted(by_peer)
    t_rows = [t_rows] + [turned(t_rows, k, k) for k in (1, 2, 3)]
    g_rows = [g_rows] + [turned(g_rows, k, k) for k in (1, 2, 3)]
    own_t, own_g = stacked(*t_rows), stacked(*g_rows)
    other_t = swapped(own_t)
    *gate_up, gate_up_mine = ring_blocks(own_t, other_t, (gate_weight, up_weight))
    other_g = swapped(own_g)
    *hgrad, hgrad_mine = ring_blocks(own_g, other_g, (down_weight,))

    near = both_ways(*gate_up[:2])
    hgrad_near = both_ways(*hgrad[:2])
    gate_up[2], gate_up[3] = after((gate_up[2], gate_up[3]), hgrad)
    low = joined(gate_up[2], near[0])
    high = joined(gate_up[3], near[1])
    far = both_ways(low, high)
    hgrad_low = joined(after(hgrad[2], low, high), hgrad_near[0])
    hgrad_high = joined(after(hgrad[3], low, high), hgrad_near[1])
    hgrad_far = both_ways(hgrad_low, hgrad_high)
    gate_up_mine = after(gate_up_mine, hgrad_low, hgrad_high)
    hidden, *factors = activations(*near, *far, gate_up_mine)
    blocks = deltas_from(hidden, *factors, *hgrad_near, *hgrad_far, hgrad_mine)
    weights = (gate_weight, up_weight, down_weight)
    low, high = blocks
    low_behind, high_ahead = both_ways(low, high)
    high_behind, low_ahead = both_ways(high, low)
    far = both_ways(low_behind, high_ahead)
    near_halves = (low, high, low_behind, high_behind, low_ahead, high_ahead)
    near, early = near_rows(near_halves, weights)
    early = swapped(early)
    first = turned(early_quarter(near, early), -2, -1)
    far_own, late = far_rows(*far, weights, near)
    sums = late_quarters(near, far_own, early, swapped(late))
    blocks = placed(after(low, sums), *near_halves[1:], *far)
    sums = [sums[0], first, turned(sums[1], -3, -2), turned(sums[2], -1, -3)]
    gate_grad, up_grad, down_grad = weight_grads(blocks, own_t, other_t, own_g, other_g, factor)
    sums[0] = after(sums[0], gate_grad)
    parts = first_exchange(collected(sums, peers))
    output, tokens_grad = totals(parts)
    return output, tokens_grad, gate_grad, up_grad, down_grad


def solution(mesh):
    placed = P(("dcn", "gx", "gz"), "gy")
    return jax.shard_map(
        per_device,
        mesh=mesh,
        in_specs=(placed,) * 5,
        out_specs=(placed,) * 5,
        check_vma=False,
    )
```

```python
import math

import jax
import jax.numpy as jnp
from jax import lax
from jax.experimental import pallas as pl
from jax.experimental.pallas import tpu as pltpu
from jax.sharding import PartitionSpec as P

BF16, F32 = jnp.bfloat16, jnp.float32
CUBE = ("dcn", "gx", "gz")
NEAR = 2
WIDTH = 512
WAYS = 4
SMEM = pl.BlockSpec(memory_space=pltpu.SMEM)
VMEM = pl.BlockSpec(memory_space=pltpu.VMEM)
PARAMS = pltpu.CompilerParams(vmem_limit_bytes=24 * 1024 * 1024)


def local(kernel, out_shape, *args, scratch=(), flops=1e6, moved=1e6):
    return pl.pallas_call(
        kernel,
        in_specs=[SMEM if a.dtype == jnp.int32 else VMEM for a in args],
        out_specs=[VMEM] * len(out_shape),
        out_shape=[jax.ShapeDtypeStruct(*s) for s in out_shape],
        scratch_shapes=list(scratch),
        compiler_params=PARAMS,
        cost_estimate=pl.CostEstimate(flops=int(flops), bytes_accessed=int(moved), transcendentals=0),
        name=kernel.__name__,
    )(*args)


def swapped(x):
    return lax.ppermute(x, "dcn", [(0, 1), (1, 0)])


def after(x, *others):
    return lax.optimization_barrier((x, *others))[0]


def copies(tokens, out_grad, peers):
    rows, width = tokens.shape

    def copies_of(t_hbm, g_hbm, out_ref, t_ref, g_ref, sems):
        moves = [
            pltpu.make_async_copy(t_hbm, t_ref, sems.at[0]),
            pltpu.make_async_copy(g_hbm, g_ref, sems.at[1]),
        ]
        for move in moves:
            move.start()
        for move in moves:
            move.wait()
        both = jnp.concatenate([t_ref[...].astype(F32), g_ref[...].astype(F32)]).astype(BF16)
        for p in range(peers):
            out_ref[p] = both

    in_hbm = pl.BlockSpec(memory_space=pltpu.HBM)
    return pl.pallas_call(
        copies_of,
        in_specs=[in_hbm] * 2,
        out_specs=VMEM,
        out_shape=jax.ShapeDtypeStruct((peers, 2 * rows, width), BF16),
        scratch_shapes=[pltpu.VMEM((rows, width), BF16)] * 2 + [pltpu.SemaphoreType.DMA((2,))],
        compiler_params=PARAMS,
        name="copies",
    )(*(pltpu.with_memory_space_constraint(x, pltpu.HBM) for x in (tokens, out_grad)))


def parted(rows_of_peers):
    peers, rows, width = rows_of_peers.shape
    half = rows // 2

    def parted_of(in_ref, t_ref, g_ref):
        for p in range(0, peers, 2):
            first, second = in_ref[p].astype(F32), in_ref[p + 1].astype(F32)
            to = slice(p * half, (p + 2) * half)
            t_ref[to] = jnp.concatenate([first[:half], second[:half]]).astype(BF16)
            g_ref[to] = jnp.concatenate([first[half:], second[half:]]).astype(BF16)

    return local(parted_of, [((peers * half, width), BF16)] * 2, rows_of_peers)


def stacked(*blocks):
    rows, width = blocks[0].shape

    def stacked_of(*refs):
        for k, ref in enumerate(refs[:-1]):
            refs[-1][k * rows : (k + 1) * rows] = ref[...]

    return local(stacked_of, [((len(blocks) * rows, width), BF16)], *blocks)[0]


def sums_into(held, first, w_ref, own_ref, other_ref):
    units, block = w_ref.shape[0], held.shape[-1]
    for half, rows_ref in enumerate((own_ref, other_ref)):
        sums = lax.dot_general(
            w_ref[...], rows_ref[...], (((1,), (1,)), ((), ())), preferred_element_type=F32
        )
        for c in range(2):
            held[2 * half + c, first : first + units] = sums[:, c * block : (c + 1) * block]


def ring_blocks(own, other, weights, earlier=()):
    count = len(weights)
    units, width = weights[0].shape
    rows = own.shape[0]
    block, part = rows // 2, count * units // 2
    first = earlier[0].shape[0] if earlier else 0

    def ring_blocks_of(own_ref, other_ref, *refs):
        w_refs, e_refs = refs[:count], refs[count : count + len(earlier)]
        low, high, forth, back, next_, before, mine, held = refs[count + len(earlier) :]
        for k, w_ref in enumerate(w_refs):
            sums_into(held, k * units, w_ref, own_ref, other_ref)
        me = lax.axis_index("gy")
        after_, far, last = (lax.rem(me + s, WAYS) for s in (1, 2, 3))
        low[...] = held[far, :part].astype(BF16)
        high[...] = held[far, part:].astype(BF16)
        for out, ref in zip((forth, back), e_refs):
            out[:first] = ref[...]
        forth[first:] = held[after_, part:].astype(BF16)
        back[first:] = held[last, :part].astype(BF16)
        next_[...] = held[after_, :part]
        before[...] = held[last, part:]
        mine[...] = held[me]

    half, full = (part, block), (2 * part, block)
    return local(
        ring_blocks_of,
        [(half, BF16)] * 2 + [((first + part, block), BF16)] * 2 + [(half, F32)] * 2 + [(full, F32)],
        own,
        other,
        *weights,
        *earlier,
        scratch=[pltpu.VMEM((WAYS,) + full, F32)],
        flops=4 * count * units * width * rows,
    )


def shifted(x, by):
    n = lax.axis_size("gy")
    return lax.ppermute(x, "gy", [(i, (i + by) % n) for i in range(n)])


def plane():
    cores, ys, zs = lax.axis_size("dcn"), lax.axis_size("gx") // NEAR, lax.axis_size("gz")
    return cores, ys, zs, lambda d, n, y, z: ((d * NEAR + n) * ys + y) * zs + z


def first_groups():
    cores, ys, zs, place = plane()
    by_z = [[place(0, n, y, z) for n in range(NEAR) for z in range(zs)] for y in range(ys)]
    by_y = [[place(1, n, y, z) for n in range(NEAR) for y in range(ys)] for z in range(zs)]
    return by_z + by_y


def first_exchange(x):
    return lax.all_to_all(x, CUBE, 0, 0, axis_index_groups=first_groups(), tiled=True)


def turned(x, by_even, by_odd):
    cores, ys, zs, place = plane()
    ways = lax.axis_size("gy")
    pairs = []
    for n in range(NEAR):
        for y in range(ys):
            for z in range(zs):
                for g in range(ways):
                    by = by_odd if g % 2 else by_even
                    for d, to in ((0, ((y + by) % ys, z)), (1, (y, (z + by) % zs))):
                        places = place(d, n, y, z), place(d, n, *to)
                        pairs.append(tuple((p // zs * ways + g) * zs + p % zs for p in places))
    return lax.ppermute(x, ("dcn", "gx", "gy", "gz"), pairs)


def joined(here, there):
    part, block = here.shape

    def joined_of(here_ref, there_ref, out_ref):
        out_ref[...] = (here_ref[...] + there_ref[...].astype(F32)).astype(BF16)

    return local(joined_of, [((part, block), BF16)], here, there)[0]


def block_sum(out, first, behind_ref, ahead_ref, low_ref, high_ref, mine_ref):
    part = low_ref.shape[0]
    direct = slice(first, first + part)
    out[:part] = mine_ref[:part] + low_ref[...].astype(F32) + ahead_ref[direct].astype(F32)
    out[part:] = mine_ref[part:] + high_ref[...].astype(F32) + behind_ref[direct].astype(F32)


def activations(*parts):
    rows, block = parts[-1].shape
    units = rows // 2

    def activations_of(behind, ahead, low, high, mine, hidden_ref, gate_ref, up_ref, total):
        block_sum(total, 0, behind, ahead, low, high, mine)
        gate, up = total[:units], total[units:]
        sigmoid = jax.nn.sigmoid(gate)
        hidden_ref[...] = (gate * sigmoid * up).astype(BF16)
        gate_ref[...] = up * sigmoid * (1.0 + gate * (1.0 - sigmoid))
        up_ref[...] = gate * sigmoid

    one = ((units, block), F32)
    return local(
        activations_of,
        [((units, block), BF16), one, one],
        *parts,
        scratch=[pltpu.VMEM((rows, block), F32)],
    )


def deltas_from(hidden, gate_factor, up_factor, *parts):
    units, block = parts[-1].shape

    def deltas_of(hidden_ref, gate_ref, up_ref, behind, ahead, low, high, mine, low_out, high_out, total):
        block_sum(total, behind.shape[0] - units // 2, behind, ahead, low, high, mine)
        rest = units // 2
        gate = (total[...] * gate_ref[...]).astype(BF16)
        low_out[:units] = hidden_ref[...]
        low_out[units:] = gate[:rest]
        high_out[:rest] = gate[rest:]
        high_out[rest:] = (total[...] * up_ref[...]).astype(BF16)

    return local(
        deltas_of,
        [((3 * units // 2, block), BF16)] * 2,
        hidden,
        gate_factor,
        up_factor,
        *parts,
        scratch=[pltpu.VMEM((units, block), F32)],
    )


def placed(*halves):
    part, block = halves[0].shape

    def placed_of(*refs):
        me, out_ref = lax.axis_index("gy"), refs[-1]
        for k, step in enumerate((0, 3, 1, 2)):
            slot = lax.rem(me + step, WAYS)
            out_ref[slot, :part] = refs[2 * k][...]
            out_ref[slot, part:] = refs[2 * k + 1][...]

    return local(placed_of, [((WAYS, 2 * part, block), BF16)], *halves)[0]


def both_ways(forth, back):
    return shifted(forth, 1), shifted(back, -1)


def early_chunk(me):
    return 3 - lax.rem(me, 2)


def rows_into(held, blocks, w_refs, store):
    gate, up, down = w_refs
    units, width = down.shape
    block = blocks[0].shape[-1]
    for k, ref in enumerate(blocks):
        for which in range(3):
            held[which, k * block : (k + 1) * block] = ref[which * units : (which + 1) * units].T
    for p in range(width // WIDTH):
        at = slice(p * WIDTH, (p + 1) * WIDTH)
        dot = lambda which, w: jnp.dot(held[which], w[:, at], preferred_element_type=F32)
        store(0, at, dot(0, down))
        store(1, at, dot(1, gate) + dot(2, up))


def near_rows(halves, weights):
    part, block = halves[0].shape
    units, width = weights[0].shape

    def near_rows_of(*refs):
        (w0, w1, w2, rows_ref, early_ref, held, *whole), halves_of = refs[6:], refs[:6]
        for k, ref in enumerate(whole):
            ref[:part] = halves_of[2 * k][...]
            ref[part:] = halves_of[2 * k + 1][...]
        me = lax.axis_index("gy")
        slots = [lax.rem(me + s, WAYS) for s in (0, 3, 1)]

        def store(kind, at, total):
            for k, slot in enumerate(slots):
                rows_ref[slot, kind, :, at] = total[k * block : (k + 1) * block]

        rows_into(held, whole, (w0, w1, w2), store)
        early_ref[...] = rows_ref[early_chunk(me)].astype(BF16)

    return local(
        near_rows_of,
        [((WAYS, 2, block, width), F32), ((2, block, width), BF16)],
        *halves,
        *weights,
        scratch=[pltpu.VMEM((3, 3 * block, units), BF16)] + [pltpu.VMEM((2 * part, block), BF16)] * 3,
        flops=18 * block * units * width,
    )


def far_rows(low, high, weights, near):
    part, block = low.shape
    units, width = weights[0].shape

    def far_rows_of(low_ref, high_ref, w0, w1, w2, near_ref, rows_ref, late_ref, held, far_block):
        me = lax.axis_index("gy")
        far_block[:part] = low_ref[...]
        far_block[part:] = high_ref[...]

        def store(kind, at, total):
            rows_ref[kind, :, at] = total

        rows_into(held, (far_block,), (w0, w1, w2), store)

        @pl.when(me < 2)
        def _():
            late_ref[...] = rows_ref[...].astype(BF16)

        @pl.when(me >= 2)
        def _():
            late_ref[...] = near_ref[me].astype(BF16)

    return local(
        far_rows_of,
        [((2, block, width), F32), ((2, block, width), BF16)],
        low,
        high,
        *weights,
        near,
        scratch=[pltpu.VMEM((3, block, units), BF16), pltpu.VMEM((2 * part, block), BF16)],
        flops=6 * block * units * width,
    )


def early_quarter(near, early):
    _, _, block, width = near.shape
    each = 2 * block // WAYS

    def early_quarter_of(near_ref, early_ref, out_ref):
        me = lax.axis_index("gy")
        odd = lax.rem(me, 2)
        at = pl.ds(pl.multiple_of(odd * each, each), each)
        for kind in range(2):
            own = near_ref[early_chunk(me) - 2, kind, at]
            out_ref[kind] = (own + early_ref[kind, at].astype(F32)).astype(BF16)

    return local(early_quarter_of, [((2, each, width), BF16)], near, early)[0]


def late_quarters(near, far, early, late):
    _, _, block, width = near.shape
    each = 2 * block // WAYS

    def late_quarters_of(near_ref, far_ref, early_ref, late_ref, mine_ref, *out_refs):
        me = lax.axis_index("gy")
        odd = lax.rem(me, 2)

        def quarter(k, kind):
            chunk, first = k * each // block, k * each % block
            at = slice(first, first + each)
            is_far, is_early = lax.rem(me + 2, WAYS) == chunk, early_chunk(me) == chunk + 2
            own = jnp.where(is_far, far_ref[kind, at], near_ref[chunk, kind, at])
            other = jnp.where(is_early, early_ref[kind, at], late_ref[kind, at])
            return own + other.astype(F32)

        for kind in range(2):
            mine_ref[kind] = quarter(0, kind)

        @pl.when(odd == 1)
        def _():
            for kind in range(2):
                for out_ref, k in zip(out_refs, (2, 3)):
                    out_ref[kind] = quarter(k, kind).astype(BF16)

        @pl.when(odd == 0)
        def _():
            for kind in range(2):
                for out_ref, k in zip(out_refs, (3, 1)):
                    out_ref[kind] = quarter(k, kind).astype(BF16)

    shape = (2, each, width)
    return local(
        late_quarters_of,
        [(shape, F32), (shape, BF16), (shape, BF16)],
        near,
        far,
        early,
        late,
    )


def collected(parts, peers):
    _, rows, width = parts[0].shape
    each = rows // peers

    def collected_of(*refs):
        for p in range(0, peers, 2):
            at = slice(p * each, (p + 2) * each)
            out, grad = refs[0][0, at], refs[0][1, at]
            for ref in refs[1:WAYS]:
                out, grad = out + ref[0, at].astype(F32), grad + ref[1, at].astype(F32)
            refs[-1][p] = jnp.concatenate([out[:each], grad[:each]]).astype(BF16)
            refs[-1][p + 1] = jnp.concatenate([out[each:], grad[each:]]).astype(BF16)

    return local(collected_of, [((peers, 2 * each, width), BF16)], *parts)[0]


def totals(parts):
    peers, rows, width = parts.shape

    def totals_of(parts_ref, out_ref, grad_ref):
        for at in range(0, width, WIDTH):
            columns = slice(at, at + WIDTH)
            total = parts_ref[0, :, columns].astype(F32)
            for p in range(1, peers):
                total += parts_ref[p, :, columns].astype(F32)
            out_ref[:, columns] = total[: rows // 2].astype(BF16)
            grad_ref[:, columns] = total[rows // 2 :].astype(BF16)

    return local(totals_of, [((rows // 2, width), BF16)] * 2, parts)


def weight_grads(blocks, own_t, other_t, own_g, other_g, factor):
    _, rows, block = blocks.shape
    units, width = rows // 3, own_t.shape[1]

    def weight_grads_of(b_ref, own_t, other_t, own_g, other_g, gate_ref, up_ref, down_ref, held):
        @pl.when(pl.program_id(0) == 0)
        def _():
            for c in range(WAYS):
                held[:, c * block : (c + 1) * block] = b_ref[c]

        for k, out_ref in enumerate((down_ref, gate_ref, up_ref)):
            own_ref, other_ref = (own_t, other_t) if k else (own_g, other_g)
            at = slice(k * units, (k + 1) * units)
            total = jnp.dot(held[at, : 2 * block], own_ref[...], preferred_element_type=F32)
            total += jnp.dot(held[at, 2 * block :], other_ref[...], preferred_element_type=F32)
            out_ref[...] = (total * factor).astype(BF16)

    token_rows = pl.BlockSpec((2 * block, WIDTH), lambda i: (0, i))
    columns = pl.BlockSpec((units, WIDTH), lambda i: (0, i))
    return pl.pallas_call(
        weight_grads_of,
        grid=(width // WIDTH,),
        in_specs=[VMEM] + [token_rows] * 4,
        out_specs=[columns] * 3,
        out_shape=[jax.ShapeDtypeStruct((units, width), BF16)] * 3,
        scratch_shapes=[pltpu.VMEM((rows, WAYS * block), BF16)],
        compiler_params=PARAMS,
        cost_estimate=pl.CostEstimate(
            flops=8 * block * rows * width, bytes_accessed=2 * rows * width, transcendentals=0
        ),
        name="weight_grads",
    )(blocks, own_t, other_t, own_g, other_g)


def per_device(tokens, gate_weight, up_weight, down_weight, out_grad):
    rows, width = tokens.shape
    factor = 1.0 / math.sqrt(rows * math.prod(lax.axis_size(axis) for axis in CUBE))

    peers = NEAR * lax.axis_size("gz")
    by_peer = first_exchange(copies(tokens, out_grad, peers))
    t_rows, g_rows = parted(by_peer)
    t_rows = [t_rows] + [turned(t_rows, k, k) for k in (1, 2, 3)]
    g_rows = [g_rows] + [turned(g_rows, k, k) for k in (1, 2, 3)]
    own_t, own_g = stacked(*t_rows), stacked(*g_rows)
    other_t = swapped(own_t)
    gate_up = ring_blocks(own_t, other_t, (gate_weight, up_weight))
    near = both_ways(*gate_up[:2])
    other_g = swapped(own_g)
    hgrad = ring_blocks(own_g, other_g, (down_weight,), gate_up[2:4])
    hgrad_near = both_ways(*hgrad[:2])
    direct = both_ways(*hgrad[2:4])

    following, before = after(tuple(gate_up[4:6]), hgrad)
    low, high = joined(following, near[0]), joined(before, near[1])
    far = both_ways(low, high)
    following, before = after(tuple(hgrad[4:6]), low, high)
    hgrad_low, hgrad_high = joined(following, hgrad_near[0]), joined(before, hgrad_near[1])
    hgrad_far = both_ways(hgrad_low, hgrad_high)
    hidden, *factors = activations(*direct, *far, gate_up[6])
    blocks = deltas_from(hidden, *factors, *direct, *hgrad_far, hgrad[6])
    weights = (gate_weight, up_weight, down_weight)
    low, high = blocks
    low_behind, high_ahead = both_ways(low, high)
    high_behind, low_ahead = both_ways(high, low)
    far = both_ways(low_behind, high_ahead)
    near_halves = (low, high, low_behind, high_behind, low_ahead, high_ahead)
    near, early = near_rows(near_halves, weights)
    early = swapped(early)
    first = turned(early_quarter(near, early), -2, -1)
    far_own, late = far_rows(*far, weights, near)
    sums = late_quarters(near, far_own, early, swapped(late))
    blocks = placed(after(low, sums), *near_halves[1:], *far)
    sums = [sums[0], first, turned(sums[1], -3, -2), turned(sums[2], -1, -3)]
    gate_grad, up_grad, down_grad = weight_grads(blocks, own_t, other_t, own_g, other_g, factor)
    sums[0] = after(sums[0], gate_grad)
    parts = first_exchange(collected(sums, peers))
    output, tokens_grad = totals(parts)
    return output, tokens_grad, gate_grad, up_grad, down_grad


def solution(mesh):
    placed = P(("dcn", "gx", "gz"), "gy")
    return jax.shard_map(
        per_device,
        mesh=mesh,
        in_specs=(placed,) * 5,
        out_specs=(placed,) * 5,
        check_vma=False,
    )
```
